32 devices in a mesh: view: 4 (over x, core), slab: 8 (over z, y).
Axes of the slice: x: 2, y: 2, z: 4, core: 2. Of those that a mesh axis runs over, the one named last changes fastest.
Arguments:
- atten: float32 [16, 350, 350], P('slab'), may hold values from 0.0005 to 0.008
- view_segment: int32 [8], P('view'), may hold values from 0 to 3
- efficiency: float32 [8, 376, 350], P('view'), may hold values from 0.5 to 2
- live_mask: int32 [8, 376, 350], P('view'), may hold values 0 or 1
Outputs:
- sensitivity: float32 [16, 350, 350], P('slab')
The draws below stay inside these ranges and needn't reach their ends.
All inputs are finite; a program needn't handle non-finite values. No bound on the sum of `live_mask` on one device may be relied on, other than what follows from the above.
Results may differ from the reference program's by a relative error of at most 0.0003.
Values sent between devices are 32-bit elements; how exact they have to be, the bound alone decides.
A program may use at most 64 MiB of HBM per device.

```python
import math
import jax
import jax.numpy as jnp
from jax import lax

NXY = 350
NSEG = 4
VIEWS = 8
NZ = 16
NA = 376


def plant(array, own_key, least, high):
    shape = array.shape
    place = [jax.random.randint(jax.random.fold_in(own_key, axis), (), 0, shape[axis]) for axis in range(len(shape))]
    array = array.at[tuple(place)].set(least)
    longest = shape.index(max(shape))
    place[longest] = (place[longest] + 1) % shape[longest]
    return array.at[tuple(place)].set(high)


def steps_of(key, extent, shards, low, high):
    def one(position, parts):
        heights = jax.random.uniform(jax.random.fold_in(jax.random.fold_in(key, 6), position), (parts,), jnp.float32, low / len(shards), high / len(shards))
        return jnp.repeat(jnp.exp(heights), extent[position] // parts).reshape((-1,) + (1,) * (len(extent) - position - 1))

    loudness = one(*shards[0])
    for cut in shards[1:]:
        loudness = loudness * one(*cut)
    return loudness


def setup_inputs(seed: int = 0) -> dict:
    streams_of = jax.random.split(jax.random.key(seed), 5)
    return {
        "atten": jnp.clip(jnp.exp(math.log(0.008) - 2.7725887 * jax.random.uniform(streams_of[0], (NZ, NXY, NXY), jnp.float32) ** steps_of(streams_of[0], (NZ, NXY, NXY), ((0, 8),), -0.2, 0.2)), 0.0005, 0.008),
        "view_segment": plant(jax.random.randint(streams_of[1], (VIEWS,), 0, NSEG), jax.random.fold_in(streams_of[1], 1), 0, NSEG - 1).astype(jnp.int32),
        "efficiency": jnp.clip(jnp.exp(math.log(2.0) - 1.3862944 * jax.random.uniform(streams_of[2], (VIEWS, NA, NXY), jnp.float32) ** steps_of(streams_of[2], (VIEWS, NA, NXY), ((0, 4),), -0.2, 0.2)), 0.5, 2.0),
        "live_mask": plant((jax.random.randint(streams_of[3], (VIEWS, NA, NXY), 0, 10) < 9).astype(jnp.int32), jax.random.fold_in(streams_of[3], 1), 0, 1),
    }


def geometry(segment):
    angle = (45.0 + 12.0 * segment.astype(jnp.float32) / (NSEG - 1)) * (math.pi / 180.0)
    slope = jnp.cos(angle) / jnp.sin(angle)
    return (slope, jnp.sqrt(1.0 + slope * slope))

def sample_index(slope, zpos):
    rows = jnp.arange(NA).astype(jnp.float32)
    centre = rows + slope * (zpos + 0.5) - NZ - 2.0
    lower = jnp.floor(centre)
    frac = centre - lower
    lower_idx = lower.astype(jnp.int32)
    upper_idx = lower_idx + 1
    lower_ok = (lower_idx >= 0) & (lower_idx < NXY)
    upper_ok = (upper_idx >= 0) & (upper_idx < NXY)
    lower_w = jnp.where(lower_ok, 1.0 - frac, 0.0)
    upper_w = jnp.where(upper_ok, frac, 0.0)
    return (jnp.clip(lower_idx, 0, NXY - 1), lower_w, jnp.clip(upper_idx, 0, NXY - 1), upper_w)

def view_project(atten, flipped, segment):
    slope, length = geometry(segment)
    source = jnp.swapaxes(atten, 1, 2) if flipped else atten

    def one_slice(total, inputs):
        plane, zpos = inputs
        lower_idx, lower_w, upper_idx, upper_w = sample_index(slope, zpos)
        first = jnp.take(plane, lower_idx, axis=0)
        second = jnp.take(plane, upper_idx, axis=0)
        return (total + lower_w[:, None] * first + upper_w[:, None] * second, None)
    zeros = jnp.zeros((NA, NXY), jnp.float32)
    total, _ = lax.scan(one_slice, zeros, (source, jnp.arange(NZ).astype(jnp.float32)))
    return length * total

def view_back(weight, flipped, segment):
    slope, length = geometry(segment)

    def one_slice(zpos):
        lower_idx, lower_w, upper_idx, upper_w = sample_index(slope, zpos)
        plane = jnp.zeros((NXY, NXY), jnp.float32)
        plane = plane.at[lower_idx].add(lower_w[:, None] * weight)
        plane = plane.at[upper_idx].add(upper_w[:, None] * weight)
        return length * plane
    back = lax.map(one_slice, jnp.arange(NZ).astype(jnp.float32))
    return jnp.swapaxes(back, 1, 2) if flipped else back

def reference(atten, view_segment, efficiency, live_mask):
    sensitivity = jnp.zeros((NZ, NXY, NXY), jnp.float32)
    for view in range(VIEWS):
        flipped = view % 2 == 1
        ray_sum = view_project(atten, flipped, view_segment[view])
        weight = efficiency[view] * live_mask[view].astype(jnp.float32) * jnp.exp(-ray_sum)
        sensitivity = sensitivity + view_back(weight, flipped, view_segment[view])
    return sensitivity
```

```python
import functools
import math

import jax
import jax.numpy as jnp
from jax import lax
from jax.experimental import pallas as pl
from jax.experimental.pallas import tpu as pltpu
from jax.sharding import PartitionSpec as P

NSEG = 4
TILE = 8
LANES = 128


def round_up(value, unit):
    return -(-value // unit) * unit


def geometry(segment, total):
    angle = (45.0 + 12.0 * segment / (NSEG - 1)) * (math.pi / 180.0)
    slope = math.cos(angle) / math.sin(angle)
    taps = []
    for z in range(total):
        centre = slope * (z + 0.5) - (total + 2.0)
        lower = math.floor(centre)
        taps.append((-lower, centre - lower))
    return math.sqrt(1.0 + slope * slope), taps


def kernel(dims, seg_ref, att_ref, eff_ref, live_ref, out_ref, nat, src, nat_e, em, slabs_in, em_in, back, image, part, other,
           sem_a, sem_ar, sem_e, sem_er, sem_b, sem_br, sem_c, sem_cr):
    S, D, N, R, L, rows, square, half = dims
    view, slab = lax.axis_index("view"), lax.axis_index("slab")
    side, flip = view // 2, view % 2

    def remote(source, target, send, recv, to_view, to_slab):
        return pltpu.make_async_remote_copy(
            src_ref=source, dst_ref=target, send_sem=send, recv_sem=recv,
            device_id=(to_view, to_slab), device_id_type=pl.DeviceIdType.MESH)

    def block(a_side, a_slab):
        return pl.ds(pl.multiple_of((a_slab * 2 + a_side) * rows, TILE), rows)

    mine = block(side, slab)
    across = 2 * (1 - side) + flip
    beside = 2 * side + 1 - flip
    corner = 2 * (1 - side) + 1 - flip

    barrier = pltpu.get_barrier_semaphore()
    count = 0
    for r in range(S):
        to_slab = lax.rem(slab + r, S)
        for to_view in ((view, across) if r else (across, beside, corner)):
            pl.semaphore_signal(barrier, inc=1, device_id=(to_view, to_slab), device_id_type=pl.DeviceIdType.MESH)
            count += 1

    nat[...] = jnp.zeros_like(nat)
    for d in range(D):
        nat[d, 0:N, 0:N] = att_ref[d]

    @pl.when(flip == 1)
    def _():
        for d in range(D):
            src[d, 0:square, :] = nat[d]

    @pl.when(flip == 0)
    def _():
        for d in range(D):
            for a in range(0, square, LANES):
                for b in range(0, square, LANES):
                    src[d, b:b + LANES, a:a + LANES] = nat[d, a:a + LANES, b:b + LANES].T
            if L > square:
                src[d, 0:square, square:L] = jnp.zeros((square, L - square), jnp.float32)

    pl.semaphore_wait(barrier, count)

    sends = []
    for r in range(1, S):
        to_slab = lax.rem(slab + r, S)
        sends.append(remote(src.at[:, block(side, to_slab), :], slabs_in.at[slab], sem_a.at[r], sem_ar.at[r], view, to_slab))
        sends[-1].start()
    slabs_in[slab] = src[:, mine, :]

    nat_e[...] = jnp.zeros_like(nat_e)
    lane = lax.broadcasted_iota(jnp.int32, (LANES, LANES), 1)
    for v in range(2):
        nat_e[0:R, 0:N] = eff_ref[v] * live_ref[v].astype(jnp.float32)
        for a in range(0, L, LANES):
            for b in range(0, square, LANES):
                turned = nat_e[a:a + LANES, b:b + LANES].T
                if a + LANES == L:
                    turned = jnp.where(lane == LANES - 1, seg_ref[v].astype(jnp.float32), turned)
                em[v, b:b + LANES, a:a + LANES] = turned
    em_sends = []
    for r in range(1, 4):
        to_view = lax.rem(view + r, 4)
        em_sends.append(remote(em.at[to_view % 2, block(to_view // 2, slab), :], em_in.at[view], sem_e.at[r], sem_er.at[r], to_view, slab))
        em_sends[-1].start()
    em_in[view] = em[flip, mine, :]

    for r in range(1, S):
        from_slab = lax.rem(slab + S - r, S)
        remote(src.at[:, mine, :], slabs_in.at[from_slab], sem_a.at[r], sem_ar.at[r], view, from_slab).wait_recv()
    for r in range(1, 4):
        from_view = lax.rem(view + 4 - r, 4)
        remote(em.at[flip, mine, :], em_in.at[from_view], sem_e.at[r], sem_er.at[r], from_view, slab).wait_recv()

    table = [geometry(g, S * D) for g in range(NSEG)]
    for t in range(0, rows, TILE):
        at = slice(t, t + TILE)
        weights = []
        for g in range(NSEG):
            length, taps = table[g]
            sums = {}
            for z, (m, f) in enumerate(taps):
                plane = slabs_in[z // D, z % D, at, :]
                for shift, coef in ((m, 1.0 - f), (m - 1, f)):
                    term = (length * coef) * plane
                    sums[shift] = sums[shift] + term if shift in sums else term
            ray = None
            for shift, value in sums.items():
                moved = pltpu.roll(value, shift, 1)
                ray = moved if ray is None else ray + moved
            gain = jnp.zeros((TILE, L), jnp.float32)
            for j in range(4):
                one = em_in[j, at, :]
                gain = gain + jnp.where(one[:, L - 1:L] == float(g), one, 0.0)
            weights.append(length * (gain * jnp.exp(-ray)))
        moved = {}

        def shifted(g, m):
            if (g, m) not in moved:
                moved[g, m] = pltpu.roll(weights[g], L - m, 1)
            return moved[g, m]

        for z in range(S * D):
            total = None
            for g in range(NSEG):
                m, f = table[g][1][z]
                term = (1.0 - f) * shifted(g, m) + f * shifted(g, m - 1)
                total = term if total is None else total + term
            back[z // D, z % D, at, :] = total

    for r in range(S):
        to_slab = lax.rem(slab + r, S)
        for e in range(2):
            if r or e:
                to_side = (side + e) % 2
                i = 2 * r + e
                sends.append(remote(back.at[to_slab, to_side], image.at[mine, :], sem_b.at[i], sem_br.at[i], 2 * to_side + flip, to_slab))
                sends[-1].start()
    image[mine, :] = back[slab, side]
    for r in range(S):
        from_slab = lax.rem(slab + S - r, S)
        for e in range(2):
            if r or e:
                from_side = (side + e) % 2
                i = 2 * r + e
                remote(back.at[slab, side], image.at[block(from_side, from_slab), :], sem_b.at[i], sem_br.at[i], 2 * from_side + flip, from_slab).wait_recv()

    @pl.when(flip == 1)
    def _():
        part[...] = image[0:square, 0:square]

    @pl.when(flip == 0)
    def _():
        for a in range(0, square, LANES):
            for b in range(0, square, LANES):
                part[b:b + LANES, a:a + LANES] = image[a:a + LANES, b:b + LANES].T

    keep = pl.ds(pl.multiple_of(flip * half, TILE), half)
    give = pl.ds(pl.multiple_of((1 - flip) * half, TILE), half)
    swap = remote(part.at[give, :], other, sem_c.at[0], sem_cr.at[0], beside, slab)
    swap.start()
    swap.wait_recv()
    out_ref[side, keep, :] = part[keep, :] + other[...]
    far = remote(out_ref.at[side, keep, :], out_ref.at[side, keep, :], sem_c.at[1], sem_cr.at[1], across, slab)
    far.start()
    near = remote(out_ref.at[side, keep, :], out_ref.at[side, keep, :], sem_c.at[2], sem_cr.at[2], beside, slab)
    near.start()
    remote(out_ref.at[side, keep, :], out_ref.at[1 - side, keep, :], sem_c.at[1], sem_cr.at[1], across, slab).wait_recv()
    last = remote(out_ref.at[1 - side, keep, :], out_ref.at[1 - side, keep, :], sem_c.at[3], sem_cr.at[3], beside, slab)
    last.start()
    remote(out_ref.at[side, keep, :], out_ref.at[side, give, :], sem_c.at[2], sem_cr.at[2], beside, slab).wait_recv()
    remote(out_ref.at[1 - side, keep, :], out_ref.at[1 - side, give, :], sem_c.at[3], sem_cr.at[3], beside, slab).wait_recv()
    for copy in sends + em_sends + [swap, far, near, last]:
        copy.wait_send()


def on_device(atten, view_segment, efficiency, live_mask):
    S = lax.axis_size("slab")
    D, N = atten.shape[0], atten.shape[1]
    R = efficiency.shape[1]
    assert lax.axis_size("view") == 4 and D == 2 and efficiency.shape[0] == 2
    L = round_up(max(R + 1, N + S * D + 3), LANES)
    square = round_up(N, LANES)
    rows = round_up(-(-N // (2 * S)), TILE)
    total_rows = max(2 * S * rows, square)
    half = round_up(N, 2 * TILE) // 2
    dims = (S, D, N, R, L, rows, square, half)
    f32 = jnp.float32
    dma = pltpu.SemaphoreType.DMA
    vmem = pl.BlockSpec(memory_space=pltpu.VMEM)
    out = pl.pallas_call(
        functools.partial(kernel, dims),
        out_shape=jax.ShapeDtypeStruct((D, 2 * half, square), f32),
        in_specs=[pl.BlockSpec(memory_space=pltpu.SMEM), vmem, vmem, vmem],
        out_specs=vmem,
        scratch_shapes=[
            pltpu.VMEM((D, square, L), f32),
            pltpu.VMEM((D, total_rows, L), f32),
            pltpu.VMEM((L, square), f32),
            pltpu.VMEM((2, total_rows, L), f32),
            pltpu.VMEM((S, D, rows, L), f32),
            pltpu.VMEM((4, rows, L), f32),
            pltpu.VMEM((S, D, rows, L), f32),
            pltpu.VMEM((total_rows, L), f32),
            pltpu.VMEM((square, square), f32),
            pltpu.VMEM((half, square), f32),
            dma((S,)), dma((S,)), dma((4,)), dma((4,)),
            dma((2 * S,)), dma((2 * S,)), dma((4,)), dma((4,)),
        ],
        compiler_params=pltpu.CompilerParams(collective_id=0, has_side_effects=True, vmem_limit_bytes=48 * 2**20),
    )(view_segment, atten, efficiency, live_mask)
    return out[:, :N, :N]


def solution(mesh):
    in_specs = (P("slab", None, None), P("view"), P("view", None, None), P("view", None, None))
    out_specs = P("slab", None, None)
    return jax.shard_map(on_device, mesh=mesh, in_specs=in_specs, out_specs=out_specs, check_vma=False)
```

```python
import functools
import math

import jax
import jax.numpy as jnp
from jax import lax
from jax.experimental import pallas as pl
from jax.experimental.pallas import tpu as pltpu
from jax.sharding import PartitionSpec as P

NSEG = 4
TILE = 8
LANES = 128
CHUNK = 16


def round_up(value, unit):
    return -(-value // unit) * unit


def geometry(segment, total):
    angle = (45.0 + 12.0 * segment / (NSEG - 1)) * (math.pi / 180.0)
    slope = math.cos(angle) / math.sin(angle)
    taps = []
    for z in range(total):
        centre = slope * (z + 0.5) - (total + 2.0)
        lower = math.floor(centre)
        taps.append((-lower, centre - lower))
    return math.sqrt(1.0 + slope * slope), taps


def kernel(dims, seg_ref, att_ref, eff_ref, live_ref, out_ref, att_v, eff_v, live_v, nat, src, em, slabs_in, em_in, mid_out, mid_in,
           weights, back, image, part, other, sem_l, sem_a, sem_ar, sem_e, sem_er, sem_m, sem_mr, sem_b, sem_br, sem_c, sem_cr):
    S, D, N, R, L, K, square, half = dims
    U = S // 2
    G = 2 * U
    chunks = -(-N // CHUNK)
    view, slab = lax.axis_index("view"), lax.axis_index("slab")
    side, flip = view // 2, view % 2
    upper, unit = slab // U, slab % U
    f32 = jnp.float32

    def group(a_side, a_unit):
        return a_unit * 2 + a_side

    def rows_of(k, g):
        return pl.ds(pl.multiple_of((k * G + g) * CHUNK, CHUNK), CHUNK)

    def guarded(k, g, act):
        if (k + 1) * G <= chunks:
            act()
        else:
            pl.when(k * G + g < chunks)(act)

    def remote(source, target, send, recv, to_view, to_slab):
        return pltpu.make_async_remote_copy(
            src_ref=source, dst_ref=target, send_sem=send, recv_sem=recv,
            device_id=(to_view, to_slab), device_id_type=pl.DeviceIdType.MESH)

    me = group(side, unit)
    across = 2 * (1 - side) + flip
    beside = 2 * side + 1 - flip
    corner = 2 * (1 - side) + 1 - flip
    partner = (1 - upper) * U + unit

    def in_half(r):
        return upper * U + lax.rem(unit + r, U)

    loads = []
    for d in range(D):
        loads.append(pltpu.make_async_copy(att_ref.at[:, d, :], att_v.at[d], sem_l.at[d]))
    for v in range(2):
        loads.append(pltpu.make_async_copy(eff_ref.at[:, v, :], eff_v.at[v], sem_l.at[D + v]))
        loads.append(pltpu.make_async_copy(live_ref.at[:, v, :], live_v.at[v], sem_l.at[D + 2 + v]))
    for load in loads:
        load.start()

    barrier = pltpu.get_barrier_semaphore()
    greet = [(view, in_half(r)) for r in range(1, U)] + [(across, in_half(r)) for r in range(U)]
    greet += [(beside, slab), (corner, slab), (view, partner)]
    for to in greet:
        pl.semaphore_signal(barrier, inc=1, device_id=to, device_id_type=pl.DeviceIdType.MESH)

    nat[...] = jnp.zeros_like(nat)
    em[...] = jnp.zeros_like(em)
    if chunks * CHUNK < image.shape[0]:
        image[chunks * CHUNK:, :] = jnp.zeros((image.shape[0] - chunks * CHUNK, L), f32)
    for d in range(D):
        loads[d].wait()
        nat[d, 0:N, 0:N] = att_v[d]

    @pl.when(flip == 1)
    def _():
        for c in range(chunks):
            for d in range(D):
                src[c % G, c // G, d] = nat[d, c * CHUNK:(c + 1) * CHUNK, :]

    @pl.when(flip == 0)
    def _():
        for b in range(0, square, LANES):
            for d in range(D):
                for a in range(0, square, LANES):
                    turned = nat[d, a:a + LANES, b:b + LANES].T
                    for i in range(0, LANES, CHUNK):
                        c = (b + i) // CHUNK
                        if c < chunks:
                            src[c % G, c // G, d, :, a:a + LANES] = turned[i:i + CHUNK, :]
        if L > square:
            for c in range(chunks):
                src[c % G, c // G, :, :, square:L] = jnp.zeros((D, CHUNK, L - square), f32)

    pl.semaphore_wait(barrier, len(greet))

    sends = []

    def send(k, g, copy):
        guarded(k, g, copy.start)
        sends.append((k, g, copy))

    for k in range(K):
        for r in range(1, U):
            g = group(side, lax.rem(unit + r, U))
            send(k, g, remote(src.at[g, k], slabs_in.at[k, unit], sem_a.at[k, r], sem_ar.at[k, r], view, in_half(r)))

        def keep_own(k=k):
            slabs_in[k, unit] = src[me, k]

        guarded(k, me, keep_own)

    lane = lax.broadcasted_iota(jnp.int32, (CHUNK, LANES), 1)
    for load in loads[D:]:
        load.wait()
    for v in range(2):
        for c in range(chunks):
            n = min(CHUNK, N - c * CHUNK)
            at = slice(c * CHUNK, c * CHUNK + n)
            em[v, c % G, c // G, 0:n, 0:R] = eff_v[v, at, :] * live_v[v, at, :].astype(f32)
            tail = em[v, c % G, c // G, :, L - LANES:L]
            em[v, c % G, c // G, :, L - LANES:L] = jnp.where(lane == LANES - 1, seg_ref[v].astype(f32), tail)
    em_sends = []
    for r in range(1, 4):
        to_view = lax.rem(view + r, 4)
        em_sends.append(remote(em.at[to_view % 2, group(to_view // 2, unit)], em_in.at[view], sem_e.at[r], sem_er.at[r], to_view, slab))
        em_sends[-1].start()
    em_in[view] = em[flip, me]

    table = [geometry(g, S * D) for g in range(NSEG)]

    def by_half(act):
        pl.when(upper == 0)(functools.partial(act, 0))
        pl.when(upper == 1)(functools.partial(act, 1))

    def project(k):
        for r in range(1, U):
            from_unit = lax.rem(unit + U - r, U)
            remote(src.at[me, k], slabs_in.at[k, from_unit], sem_a.at[k, r], sem_ar.at[k, r], view, upper * U + from_unit).wait_recv()

        def act(h):
            for t in range(0, CHUNK, TILE):
                at = slice(t, t + TILE)
                for g in range(NSEG):
                    length, taps = table[g]
                    sums = {}
                    for n in range(U * D):
                        m, f = taps[h * U * D + n]
                        plane = slabs_in[k, n // D, n % D, at, :]
                        for shift, coef in ((m, 1.0 - f), (m - 1, f)):
                            term = (length * coef) * plane
                            sums[shift] = sums[shift] + term if shift in sums else term
                    ray = None
                    for shift, value in sums.items():
                        moved = pltpu.roll(value, shift, 1)
                        ray = moved if ray is None else ray + moved
                    mid_out[k, g, at, :] = ray

        by_half(act)

    def mid(k):
        return remote(mid_out.at[k], mid_in.at[k], sem_m.at[k], sem_mr.at[k], view, partner)

    def back_project(k):
        mid(k).wait_recv()
        for t in range(0, CHUNK, TILE):
            at = slice(t, t + TILE)
            for g in range(NSEG):
                gain = jnp.zeros((TILE, L), f32)
                for j in range(4):
                    one = em_in[j, k, at, :]
                    gain = gain + jnp.where(one[:, L - 1:L] == float(g), one, 0.0)
                weights[g, at, :] = table[g][0] * (gain * jnp.exp(-(mid_out[k, g, at, :] + mid_in[k, g, at, :])))

        def act(h):
            for t in range(0, CHUNK, TILE):
                at = slice(t, t + TILE)
                moved = {}

                def shifted(g, m):
                    if (g, m) not in moved:
                        moved[g, m] = pltpu.roll(weights[g, at, :], L - m, 1)
                    return moved[g, m]

                for n in range(U * D):
                    total = None
                    for g in range(NSEG):
                        m, f = table[g][1][h * U * D + n]
                        term = (1.0 - f) * shifted(g, m) + f * shifted(g, m - 1)
                        total = term if total is None else total + term
                    back[k, n // D, n % D, at, :] = total

        by_half(act)
        image[rows_of(k, me), :] = back[k, unit, side]

    def finish(k):
        guarded(k, me, functools.partial(back_project, k))
        for r in range(U):
            to_unit = lax.rem(unit + r, U)
            for e in range(2):
                if r or e:
                    to_side = (side + e) % 2
                    i = 2 * r + e
                    send(k, me, remote(back.at[k, to_unit, to_side], image.at[rows_of(k, me), :], sem_b.at[k, i], sem_br.at[k, i],
                                       2 * to_side + flip, in_half(r)))

    for k in range(K):
        guarded(k, me, functools.partial(project, k))
        send(k, me, mid(k))
        if k == 0:
            for r in range(1, 4):
                from_view = lax.rem(view + 4 - r, 4)
                remote(em.at[flip, me], em_in.at[from_view], sem_e.at[r], sem_er.at[r], from_view, slab).wait_recv()
        else:
            finish(k - 1)
    finish(K - 1)

    def arrive(k):
        for r in range(U):
            from_unit = lax.rem(unit + U - r, U)
            for e in range(2):
                if r or e:
                    from_side = (side + e) % 2
                    i = 2 * r + e
                    g = group(from_side, from_unit)
                    copy = remote(back.at[k, unit, side], image.at[rows_of(k, g), :], sem_b.at[k, i], sem_br.at[k, i],
                                  2 * from_side + flip, upper * U + from_unit)
                    guarded(k, g, copy.wait_recv)

    arrived = 0
    for a in range(0, square, LANES):
        while arrived < K and arrived * G * CHUNK < a + LANES:
            arrive(arrived)
            arrived += 1

        @pl.when(flip == 1)
        def _():
            part[a:a + LANES, :] = image[a:a + LANES, 0:square]

        @pl.when(flip == 0)
        def _():
            for b in range(0, square, LANES):
                part[b:b + LANES, a:a + LANES] = image[a:a + LANES, b:b + LANES].T

    keep = pl.ds(pl.multiple_of(flip * half, TILE), half)
    give = pl.ds(pl.multiple_of((1 - flip) * half, TILE), half)
    swap = remote(part.at[give, :], other, sem_c.at[0], sem_cr.at[0], beside, slab)
    swap.start()
    swap.wait_recv()
    out_ref[side, keep, :] = part[keep, :] + other[...]
    far = remote(out_ref.at[side, keep, :], out_ref.at[side, keep, :], sem_c.at[1], sem_cr.at[1], across, slab)
    far.start()
    near = remote(out_ref.at[side, keep, :], out_ref.at[side, keep, :], sem_c.at[2], sem_cr.at[2], beside, slab)
    near.start()
    remote(out_ref.at[side, keep, :], out_ref.at[1 - side, keep, :], sem_c.at[1], sem_cr.at[1], across, slab).wait_recv()
    last = remote(out_ref.at[1 - side, keep, :], out_ref.at[1 - side, keep, :], sem_c.at[3], sem_cr.at[3], beside, slab)
    last.start()
    remote(out_ref.at[side, keep, :], out_ref.at[side, give, :], sem_c.at[2], sem_cr.at[2], beside, slab).wait_recv()
    remote(out_ref.at[1 - side, keep, :], out_ref.at[1 - side, give, :], sem_c.at[3], sem_cr.at[3], beside, slab).wait_recv()
    for k, g, copy in sends:
        guarded(k, g, copy.wait_send)
    for copy in em_sends + [swap, far, near, last]:
        copy.wait_send()


def on_device(atten, view_segment, efficiency, live_mask):
    S = lax.axis_size("slab")
    D, N = atten.shape[0], atten.shape[1]
    R = efficiency.shape[1]
    assert lax.axis_size("view") == 4 and D == 2 and efficiency.shape[0] == 2 and S % 2 == 0
    L = round_up(max(R + 1, N + S * D + 3), LANES)
    square = round_up(N, LANES)
    U = S // 2
    G = 2 * U
    K = -(-N // (G * CHUNK))
    half = round_up(N, 2 * TILE) // 2
    dims = (S, D, N, R, L, K, square, half)
    f32 = jnp.float32
    dma = pltpu.SemaphoreType.DMA
    vmem = pl.BlockSpec(memory_space=pltpu.VMEM)
    anywhere = pl.BlockSpec(memory_space=pl.ANY)
    out = pl.pallas_call(
        functools.partial(kernel, dims),
        out_shape=jax.ShapeDtypeStruct((D, 2 * half, square), f32),
        in_specs=[pl.BlockSpec(memory_space=pltpu.SMEM), anywhere, anywhere, anywhere],
        out_specs=vmem,
        scratch_shapes=[
            pltpu.VMEM((D, N, N), f32),
            pltpu.VMEM((2, N, R), f32),
            pltpu.VMEM((2, N, R), jnp.int32),
            pltpu.VMEM((D, square, L), f32),
            pltpu.VMEM((G, K, D, CHUNK, L), f32),
            pltpu.VMEM((2, G, K, CHUNK, L), f32),
            pltpu.VMEM((K, U, D, CHUNK, L), f32),
            pltpu.VMEM((4, K, CHUNK, L), f32),
            pltpu.VMEM((K, NSEG, CHUNK, L), f32),
            pltpu.VMEM((K, NSEG, CHUNK, L), f32),
            pltpu.VMEM((NSEG, CHUNK, L), f32),
            pltpu.VMEM((K, U, D, CHUNK, L), f32),
            pltpu.VMEM((max(K * G * CHUNK, square), L), f32),
            pltpu.VMEM((square, square), f32),
            pltpu.VMEM((half, square), f32),
            dma((D + 4,)),
            dma((K, U)), dma((K, U)), dma((4,)), dma((4,)),
            dma((K,)), dma((K,)), dma((K, G)), dma((K, G)), dma((4,)), dma((4,)),
        ],
        compiler_params=pltpu.CompilerParams(collective_id=0, has_side_effects=True, vmem_limit_bytes=48 * 2**20),
    )(view_segment, jnp.transpose(atten, (1, 0, 2)), jnp.transpose(efficiency, (2, 0, 1)), jnp.transpose(live_mask, (2, 0, 1)))
    return out[:, :N, :N]


def solution(mesh):
    in_specs = (P("slab", None, None), P("view"), P("view", None, None), P("view", None, None))
    out_specs = P("slab", None, None)
    return jax.shard_map(on_device, mesh=mesh, in_specs=in_specs, out_specs=out_specs, check_vma=False)
```

```python
import functools
import math

import jax
import jax.numpy as jnp
from jax import lax
from jax.experimental import pallas as pl
from jax.experimental.pallas import tpu as pltpu
from jax.sharding import PartitionSpec as P

NSEG = 4
TILE = 8
LANES = 128
CHUNK = 16


def round_up(value, unit):
    return -(-value // unit) * unit


def geometry(segment, total):
    angle = (45.0 + 12.0 * segment / (NSEG - 1)) * (math.pi / 180.0)
    slope = math.cos(angle) / math.sin(angle)
    taps = []
    for z in range(total):
        centre = slope * (z + 0.5) - (total + 2.0)
        lower = math.floor(centre)
        taps.append((-lower, centre - lower))
    return math.sqrt(1.0 + slope * slope), taps


def kernel(dims, seg_ref, att_ref, eff_ref, live_ref, out_ref, att_v, eff_v, live_v, nat, src, em, slabs_in, em_in, mid_out, mid_in,
           weights, back, image, part, other, sem_l, sem_a, sem_ar, sem_e, sem_er, sem_m, sem_mr, sem_b, sem_br,
           sem_s, sem_sr, sem_f, sem_fr, sem_n, sem_nr, sem_t, sem_tr):
    S, D, N, R, L, K, square, half = dims
    U = S // 2
    G = 2 * U
    chunks = -(-N // CHUNK)
    view, slab = lax.axis_index("view"), lax.axis_index("slab")
    side, flip = view // 2, view % 2
    upper, unit = slab // U, slab % U
    f32 = jnp.float32

    def group(a_side, a_unit):
        return a_unit * 2 + a_side

    def rows_of(k, g):
        return pl.ds(pl.multiple_of((k * G + g) * CHUNK, CHUNK), CHUNK)

    def guarded(k, g, act):
        if (k + 1) * G <= chunks:
            act()
        else:
            pl.when(k * G + g < chunks)(act)

    def remote(source, target, send, recv, to_view, to_slab):
        return pltpu.make_async_remote_copy(
            src_ref=source, dst_ref=target, send_sem=send, recv_sem=recv,
            device_id=(to_view, to_slab), device_id_type=pl.DeviceIdType.MESH)

    me = group(side, unit)
    across = 2 * (1 - side) + flip
    beside = 2 * side + 1 - flip
    corner = 2 * (1 - side) + 1 - flip
    partner = (1 - upper) * U + unit

    def in_half(r):
        return upper * U + lax.rem(unit + r, U)

    loads = []
    for d in range(D):
        loads.append(pltpu.make_async_copy(att_ref.at[:, d, :], att_v.at[d], sem_l.at[d]))
    for v in range(2):
        loads.append(pltpu.make_async_copy(eff_ref.at[:, v, :], eff_v.at[v], sem_l.at[D + v]))
        loads.append(pltpu.make_async_copy(live_ref.at[:, v, :], live_v.at[v], sem_l.at[D + 2 + v]))
    for load in loads:
        load.start()

    barrier = pltpu.get_barrier_semaphore()
    greet = [(view, in_half(r)) for r in range(1, U)] + [(across, in_half(r)) for r in range(U)]
    greet += [(beside, slab), (corner, slab), (view, partner)]
    for to in greet:
        pl.semaphore_signal(barrier, inc=1, device_id=to, device_id_type=pl.DeviceIdType.MESH)

    nat[...] = jnp.zeros_like(nat)
    src[...] = jnp.zeros_like(src)
    em[...] = jnp.zeros_like(em)
    if chunks * CHUNK < image.shape[0]:
        image[chunks * CHUNK:, :] = jnp.zeros((image.shape[0] - chunks * CHUNK, L), f32)
    for d in range(D):
        loads[d].wait()

    @pl.when(flip == 0)
    def _():
        for d in range(D):
            nat[d, 0:N, 0:N] = att_v[d]

    pl.semaphore_wait(barrier, len(greet))

    sends = []

    def send(k, g, copy):
        guarded(k, g, copy.start)
        sends.append((k, g, copy))

    started = 0
    for b in range(0, square, LANES):
        inside = range(b // CHUNK, min((b + LANES) // CHUNK, chunks))

        @pl.when(flip == 1)
        def _():
            for c in inside:
                n = min(CHUNK, N - c * CHUNK)
                for d in range(D):
                    src[c % G, c // G, d, 0:n, 0:N] = att_v[d, c * CHUNK:c * CHUNK + n, :]

        @pl.when(flip == 0)
        def _():
            for d in range(D):
                for a in range(0, square, LANES):
                    turned = nat[d, a:a + LANES, b:b + LANES].T
                    for c in inside:
                        src[c % G, c // G, d, :, a:a + LANES] = turned[c * CHUNK - b:(c + 1) * CHUNK - b, :]

        while started < K and ((started + 1) * G * CHUNK <= b + LANES or b + LANES == square):
            k = started
            for r in range(1, U):
                g = group(side, lax.rem(unit + r, U))
                send(k, g, remote(src.at[g, k], slabs_in.at[k, unit], sem_a.at[k, r], sem_ar.at[k, r], view, in_half(r)))

            def keep_own(k=k):
                slabs_in[k, unit] = src[me, k]

            guarded(k, me, keep_own)
            started += 1

    lane = lax.broadcasted_iota(jnp.int32, (CHUNK, LANES), 1)
    for load in loads[D:]:
        load.wait()
    for v in range(2):
        for c in range(chunks):
            n = min(CHUNK, N - c * CHUNK)
            at = slice(c * CHUNK, c * CHUNK + n)
            em[v, c % G, c // G, 0:n, 0:R] = eff_v[v, at, :] * live_v[v, at, :].astype(f32)
            tail = em[v, c % G, c // G, :, L - LANES:L]
            em[v, c % G, c // G, :, L - LANES:L] = jnp.where(lane == LANES - 1, seg_ref[v].astype(f32), tail)
    em_sends = []
    for r in range(1, 4):
        to_view = lax.rem(view + r, 4)
        em_sends.append(remote(em.at[to_view % 2, group(to_view // 2, unit)], em_in.at[view], sem_e.at[r], sem_er.at[r], to_view, slab))
        em_sends[-1].start()
    em_in[view] = em[flip, me]

    table = [geometry(g, S * D) for g in range(NSEG)]

    def by_half(act):
        pl.when(upper == 0)(functools.partial(act, 0))
        pl.when(upper == 1)(functools.partial(act, 1))

    def project(k):
        for r in range(1, U):
            from_unit = lax.rem(unit + U - r, U)
            remote(src.at[me, k], slabs_in.at[k, from_unit], sem_a.at[k, r], sem_ar.at[k, r], view, upper * U + from_unit).wait_recv()

        def act(h):
            for t in range(0, CHUNK, TILE):
                at = slice(t, t + TILE)
                for g in range(NSEG):
                    length, taps = table[g]
                    sums = {}
                    for n in range(U * D):
                        m, f = taps[h * U * D + n]
                        plane = slabs_in[k, n // D, n % D, at, :]
                        for shift, coef in ((m, 1.0 - f), (m - 1, f)):
                            term = (length * coef) * plane
                            sums[shift] = sums[shift] + term if shift in sums else term
                    ray = None
                    for shift, value in sums.items():
                        moved = pltpu.roll(value, shift, 1)
                        ray = moved if ray is None else ray + moved
                    mid_out[k, g, at, :] = ray

        by_half(act)

    def mid(k):
        return remote(mid_out.at[k], mid_in.at[k], sem_m.at[k], sem_mr.at[k], view, partner)

    def back_project(k):
        mid(k).wait_recv()
        for t in range(0, CHUNK, TILE):
            at = slice(t, t + TILE)
            for g in range(NSEG):
                gain = jnp.zeros((TILE, L), f32)
                for j in range(4):
                    one = em_in[j, k, at, :]
                    gain = gain + jnp.where(one[:, L - 1:L] == float(g), one, 0.0)
                weights[g, at, :] = table[g][0] * (gain * jnp.exp(-(mid_out[k, g, at, :] + mid_in[k, g, at, :])))

        def act(h):
            for t in range(0, CHUNK, TILE):
                at = slice(t, t + TILE)
                moved = {}

                def shifted(g, m):
                    if (g, m) not in moved:
                        moved[g, m] = pltpu.roll(weights[g, at, :], L - m, 1)
                    return moved[g, m]

                for n in range(U * D):
                    total = None
                    for g in range(NSEG):
                        m, f = table[g][1][h * U * D + n]
                        term = (1.0 - f) * shifted(g, m) + f * shifted(g, m - 1)
                        total = term if total is None else total + term
                    back[k, n // D, n % D, at, :] = total

        by_half(act)
        image[rows_of(k, me), :] = back[k, unit, side]

    def finish(k):
        guarded(k, me, functools.partial(back_project, k))
        for r in range(U):
            to_unit = lax.rem(unit + r, U)
            for e in range(2):
                if r or e:
                    to_side = (side + e) % 2
                    i = 2 * r + e
                    send(k, me, remote(back.at[k, to_unit, to_side], image.at[rows_of(k, me), :], sem_b.at[k, i], sem_br.at[k, i],
                                       2 * to_side + flip, in_half(r)))

    def arrive(k):
        for r in range(U):
            from_unit = lax.rem(unit + U - r, U)
            for e in range(2):
                if r or e:
                    from_side = (side + e) % 2
                    i = 2 * r + e
                    g = group(from_side, from_unit)
                    copy = remote(back.at[k, unit, side], image.at[rows_of(k, g), :], sem_b.at[k, i], sem_br.at[k, i],
                                  2 * from_side + flip, upper * U + from_unit)
                    guarded(k, g, copy.wait_recv)

    bands = square // LANES
    split = square - LANES
    regions = (
        ((0, half, 0, split, 0), (0, half, split, square, 1)),
        ((half, split, 0, split, 0), (half, split, split, square, 1), (split, 2 * half, 0, square, 1)),
    )
    shared = [min((a + 1) * LANES, half) - a * LANES for a in range(bands) if a * LANES < half]

    def swap(f, a):
        if f == 0:
            lanes = slice(a * LANES, (a + 1) * LANES)
            return remote(part.at[half:2 * half, lanes], other.at[:, lanes], sem_s.at[a], sem_sr.at[a], beside, slab)
        at = slice(a * LANES, a * LANES + shared[a])
        return remote(image.at[at, 0:square], other.at[at, :], sem_s.at[a], sem_sr.at[a], beside, slab)

    def spread(f, i, a_side, sems, to_view):
        r0, r1, l0, l1, _ = regions[f][i]
        place = out_ref.at[a_side, r0:r1, l0:l1]
        return remote(place, place, sems[0].at[i], sems[1].at[i], to_view, slab)

    far_sems, near_sems, last_sems = (sem_f, sem_fr), (sem_n, sem_nr), (sem_t, sem_tr)

    def band(f, a):
        if f == 0:
            for b in range(0, square, LANES):
                part[b:b + LANES, a * LANES:(a + 1) * LANES] = image[a * LANES:(a + 1) * LANES, b:b + LANES].T
            swap(0, a).start()
        elif a < len(shared):
            swap(1, a).start()
        if a < bands - 2:
            return
        stage = a - (bands - 2)
        if f == 1:
            for n in range(bands - 1) if stage == 0 else (bands - 1,):
                swap(0, n).wait_recv()
        elif stage == 0:
            for n in range(len(shared)):
                swap(1, n).wait_recv()
        for i, (r0, r1, l0, l1, when) in enumerate(regions[f]):
            if when == stage:
                own = part if f == 0 else image
                out_ref[side, r0:r1, l0:l1] = own[r0:r1, l0:l1] + other[r0 - f * half:r1 - f * half, l0:l1]
                spread(f, i, side, far_sems, across).start()
                spread(f, i, side, near_sems, beside).start()

    def settle(f):
        for i in range(len(regions[f])):
            spread(f, i, 1 - side, far_sems, across).wait_recv()
            spread(f, i, 1 - side, last_sems, beside).start()
        for i in range(len(regions[1 - f])):
            spread(1 - f, i, side, near_sems, beside).wait_recv()
        for i in range(len(regions[1 - f])):
            spread(1 - f, i, 1 - side, last_sems, beside).wait_recv()
        for a in range(bands if f == 0 else len(shared)):
            swap(f, a).wait_send()
        for i in range(len(regions[f])):
            spread(f, i, side, far_sems, across).wait_send()
            spread(f, i, side, near_sems, beside).wait_send()
            spread(f, i, 1 - side, last_sems, beside).wait_send()

    progress = {"arrived": 0, "band": 0}

    def ready(k):
        while progress["arrived"] <= k:
            arrive(progress["arrived"])
            progress["arrived"] += 1
        while progress["band"] < bands and (k == K - 1 or (progress["band"] + 1) * LANES <= (k + 1) * G * CHUNK):
            for f in range(2):
                pl.when(flip == f)(functools.partial(band, f, progress["band"]))
            progress["band"] += 1

    for k in range(K):
        guarded(k, me, functools.partial(project, k))
        send(k, me, mid(k))
        if k == 0:
            for r in range(1, 4):
                from_view = lax.rem(view + 4 - r, 4)
                remote(em.at[flip, me], em_in.at[from_view], sem_e.at[r], sem_er.at[r], from_view, slab).wait_recv()
        else:
            finish(k - 1)
    if K > 1:
        ready(K - 2)
    finish(K - 1)
    ready(K - 1)
    for f in range(2):
        pl.when(flip == f)(functools.partial(settle, f))
    for k, g, copy in sends:
        guarded(k, g, copy.wait_send)
    for copy in em_sends:
        copy.wait_send()


def on_device(atten, view_segment, efficiency, live_mask):
    S = lax.axis_size("slab")
    D, N = atten.shape[0], atten.shape[1]
    R = efficiency.shape[1]
    assert lax.axis_size("view") == 4 and D == 2 and efficiency.shape[0] == 2 and S % 2 == 0
    L = round_up(max(R + 1, N + S * D + 3), LANES)
    square = round_up(N, LANES)
    U = S // 2
    G = 2 * U
    K = -(-N // (G * CHUNK))
    half = round_up(N, 2 * TILE) // 2
    dims = (S, D, N, R, L, K, square, half)
    f32 = jnp.float32
    dma = pltpu.SemaphoreType.DMA
    vmem = pl.BlockSpec(memory_space=pltpu.VMEM)
    far = pl.BlockSpec(memory_space=pl.ANY)
    out = pl.pallas_call(
        functools.partial(kernel, dims),
        out_shape=jax.ShapeDtypeStruct((D, 2 * half, square), f32),
        in_specs=[pl.BlockSpec(memory_space=pltpu.SMEM), far, far, far],
        out_specs=vmem,
        scratch_shapes=[
            pltpu.VMEM((D, N, N), f32),
            pltpu.VMEM((2, N, R), f32),
            pltpu.VMEM((2, N, R), jnp.int32),
            pltpu.VMEM((D, square, L), f32),
            pltpu.VMEM((G, K, D, CHUNK, L), f32),
            pltpu.VMEM((2, G, K, CHUNK, L), f32),
            pltpu.VMEM((K, U, D, CHUNK, L), f32),
            pltpu.VMEM((4, K, CHUNK, L), f32),
            pltpu.VMEM((K, NSEG, CHUNK, L), f32),
            pltpu.VMEM((K, NSEG, CHUNK, L), f32),
            pltpu.VMEM((NSEG, CHUNK, L), f32),
            pltpu.VMEM((K, U, D, CHUNK, L), f32),
            pltpu.VMEM((max(K * G * CHUNK, square), L), f32),
            pltpu.VMEM((square, square), f32),
            pltpu.VMEM((half, square), f32),
            dma((D + 4,)),
            dma((K, U)), dma((K, U)), dma((4,)), dma((4,)),
            dma((K,)), dma((K,)), dma((K, G)), dma((K, G)),
            dma((square // LANES,)), dma((square // LANES,)), *[dma((3,))] * 6,
        ],
        compiler_params=pltpu.CompilerParams(collective_id=0, has_side_effects=True, vmem_limit_bytes=63 * 2**20),
    )(view_segment, jnp.transpose(atten, (1, 0, 2)), jnp.transpose(efficiency, (2, 0, 1)), jnp.transpose(live_mask, (2, 0, 1)))
    return out[:, :N, :N]


def solution(mesh):
    in_specs = (P("slab", None, None), P("view"), P("view", None, None), P("view", None, None))
    out_specs = P("slab", None, None)
    return jax.shard_map(on_device, mesh=mesh, in_specs=in_specs, out_specs=out_specs, check_vma=False)
```

```python
import functools
import math

import jax
import jax.numpy as jnp
from jax import lax
from jax.experimental import pallas as pl
from jax.experimental.pallas import tpu as pltpu
from jax.sharding import PartitionSpec as P

NSEG = 4
TILE = 8
LANES = 128
CHUNK = 16


def round_up(value, unit):
    return -(-value // unit) * unit


def geometry(segment, total):
    angle = (45.0 + 12.0 * segment / (NSEG - 1)) * (math.pi / 180.0)
    slope = math.cos(angle) / math.sin(angle)
    taps = []
    for z in range(total):
        centre = slope * (z + 0.5) - (total + 2.0)
        lower = math.floor(centre)
        taps.append((-lower, centre - lower))
    return math.sqrt(1.0 + slope * slope), taps


def kernel(dims, seg_ref, att_ref, eff_ref, live_ref, out_ref, att_v, eff_v, live_v, nat, src, em, slabs_in, em_in, mid_out, mid_in,
           weights, back, image, part, other, whole, sem_l, sem_a, sem_ar, sem_e, sem_er, sem_m, sem_mr, sem_b, sem_br,
           sem_s, sem_sr, sem_f, sem_fr, sem_n, sem_nr, sem_t, sem_tr, sem_w):
    S, D, N, R, L, K, square, half = dims
    U = S // 2
    G = 2 * U
    chunks = -(-N // CHUNK)
    view, slab = lax.axis_index("view"), lax.axis_index("slab")
    side, flip = view // 2, view % 2
    upper, unit = slab // U, slab % U
    f32 = jnp.float32

    def group(a_side, a_unit):
        return a_unit * 2 + a_side

    def rows_of(k, g):
        return pl.ds(pl.multiple_of((k * G + g) * CHUNK, CHUNK), CHUNK)

    def guarded(k, g, act):
        if isinstance(k, int) and (k + 1) * G <= chunks:
            act()
        else:
            pl.when(k * G + g < chunks)(act)

    def remote(source, target, send, recv, to_view, to_slab):
        return pltpu.make_async_remote_copy(
            src_ref=source, dst_ref=target, send_sem=send, recv_sem=recv,
            device_id=(to_view, to_slab), device_id_type=pl.DeviceIdType.MESH)

    me = group(side, unit)
    across = 2 * (1 - side) + flip
    beside = 2 * side + 1 - flip
    corner = 2 * (1 - side) + 1 - flip
    partner = (1 - upper) * U + unit

    def in_half(r):
        return upper * U + lax.rem(unit + r, U)

    loads = []
    for d in range(D):
        loads.append(pltpu.make_async_copy(att_ref.at[:, d, :], att_v.at[d], sem_l.at[d]))
        loads[-1].start()
    for v in range(2):
        loads.append(pltpu.make_async_copy(eff_ref.at[:, v, :], eff_v.at[v], sem_l.at[D + v]))
        loads.append(pltpu.make_async_copy(live_ref.at[:, v, :], live_v.at[v], sem_l.at[D + 2 + v]))

    barrier = pltpu.get_barrier_semaphore()
    greet = [(view, in_half(r)) for r in range(1, U)] + [(across, in_half(r)) for r in range(U)]
    greet += [(beside, slab), (corner, slab), (view, partner)]
    for to in greet:
        pl.semaphore_signal(barrier, inc=1, device_id=to, device_id_type=pl.DeviceIdType.MESH)

    def zero_rows(i, carry):
        nat[i // (square // TILE), pl.ds(pl.multiple_of(i % (square // TILE) * TILE, TILE), TILE), :] = jnp.zeros((TILE, L), f32)
        return carry

    lax.fori_loop(0, D * square // TILE, zero_rows, 0)
    if L > square:
        src[:, :, :, :, square:L] = jnp.zeros((*src.shape[:4], L - square), f32)
    if chunks * CHUNK < image.shape[0]:
        image[chunks * CHUNK:, :] = jnp.zeros((image.shape[0] - chunks * CHUNK, L), f32)
    for d in range(D):
        loads[d].wait()
    for load in loads[D:]:
        load.start()
    for d in range(D):
        nat[d, 0:N, 0:N] = att_v[d]

    pl.semaphore_wait(barrier, len(greet))

    def outgoing(k, r):
        to_unit = lax.rem(unit + r, U)
        g = group(side, to_unit)
        return g, remote(src.at[g, k], slabs_in.at[k, unit], sem_a.at[k, r], sem_ar.at[k, r], view, upper * U + to_unit)

    per_band = LANES // CHUNK
    started = 0
    for b in range(0, square, LANES):
        first = b // CHUNK

        @pl.when(flip == 1)
        def _():
            def act(i, carry):
                c = first + i
                src[c % G, c // G] = nat[:, pl.ds(pl.multiple_of(c * CHUNK, CHUNK), CHUNK), :]
                return carry

            lax.fori_loop(0, per_band, act, 0)

        @pl.when(flip == 0)
        def _():
            def act(d, carry):
                for a in range(0, square, LANES):
                    turned = nat[d, a:a + LANES, b:b + LANES].T
                    for i in range(per_band):
                        c = first + i
                        src[c % G, c // G, d, :, a:a + LANES] = turned[i * CHUNK:(i + 1) * CHUNK, :]
                return carry

            lax.fori_loop(0, D, act, 0)

        while started < K and ((started + 1) * G * CHUNK <= b + LANES or b + LANES == square):
            k = started
            for r in range(1, U):
                g, copy = outgoing(k, r)
                guarded(k, g, copy.start)

            def keep_own(k=k):
                slabs_in[k, unit] = src[me, k]

            guarded(k, me, keep_own)
            started += 1

    lane = lax.broadcasted_iota(jnp.int32, (CHUNK, LANES), 1)
    for load in loads[D:]:
        load.wait()
    clear = R // LANES * LANES
    for v in range(2):
        tail = jnp.where(lane == LANES - 1, seg_ref[v].astype(f32), 0.0)

        def blank(c, v=v, tail=tail):
            for a in range(clear, L, LANES):
                em[v, c % G, c // G, :, a:a + LANES] = tail if a + LANES == L else jnp.zeros((CHUNK, LANES), f32)

        def fill(c, carry, v=v, blank=blank):
            blank(c)
            at = pl.ds(pl.multiple_of(c * CHUNK, CHUNK), CHUNK)
            em[v, c % G, c // G, :, 0:R] = eff_v[v, at, :] * live_v[v, at, :].astype(f32)
            return carry

        lax.fori_loop(0, N // CHUNK, fill, 0)
        for c in range(N // CHUNK, K * G):
            n = N - c * CHUNK
            if n > 0:
                blank(c)
                em[v, c % G, c // G, 0:n, 0:R] = eff_v[v, c * CHUNK:N, :] * live_v[v, c * CHUNK:N, :].astype(f32)
                if n < CHUNK:
                    em[v, c % G, c // G, n:, :] = jnp.zeros((CHUNK - n, L), f32)
            else:
                em[v, c % G, c // G] = jnp.zeros((CHUNK, L), f32)
    em_sends = []
    for r in range(1, 4):
        to_view = lax.rem(view + r, 4)
        em_sends.append(remote(em.at[to_view % 2, group(to_view // 2, unit)], em_in.at[view], sem_e.at[r], sem_er.at[r], to_view, slab))
        em_sends[-1].start()
    em_in[view] = em[flip, me]

    table = [geometry(g, S * D) for g in range(NSEG)]

    def tiles(act):
        def step(t, carry):
            act(pl.ds(pl.multiple_of(t * TILE, TILE), TILE))
            return carry

        if CHUNK == TILE:
            act(slice(0, TILE))
        else:
            lax.fori_loop(0, CHUNK // TILE, step, 0)

    def by_half(act):
        pl.when(upper == 0)(functools.partial(act, 0))
        pl.when(upper == 1)(functools.partial(act, 1))

    def project(k):
        for r in range(1, U):
            from_unit = lax.rem(unit + U - r, U)
            remote(src.at[me, k], slabs_in.at[k, from_unit], sem_a.at[k, r], sem_ar.at[k, r], view, upper * U + from_unit).wait_recv()

        def act(h):
            @tiles
            def _(at):
                for g in range(NSEG):
                    length, taps = table[g]
                    sums = {}
                    for n in range(U * D):
                        m, f = taps[h * U * D + n]
                        plane = slabs_in[k, n // D, n % D, at, :]
                        for shift, coef in ((m, 1.0 - f), (m - 1, f)):
                            term = (length * coef) * plane
                            sums[shift] = sums[shift] + term if shift in sums else term
                    ray = None
                    for shift, value in sums.items():
                        moved = pltpu.roll(value, shift, 1)
                        ray = moved if ray is None else ray + moved
                    mid_out[k, g, at, :] = ray

        by_half(act)

    def mid(k):
        return remote(mid_out.at[k], mid_in.at[k], sem_m.at[k], sem_mr.at[k], view, partner)

    def back_project(k):
        mid(k).wait_recv()
        @tiles
        def _(at):
            for g in range(NSEG):
                gain = jnp.zeros((TILE, L), f32)
                for j in range(4):
                    one = em_in[j, k, at, :]
                    gain = gain + jnp.where(one[:, L - 1:L] == float(g), one, 0.0)
                weights[g, at, :] = table[g][0] * (gain * jnp.exp(-(mid_out[k, g, at, :] + mid_in[k, g, at, :])))

        def act(h):
            @tiles
            def _(at):
                moved = {}

                def shifted(g, m):
                    if (g, m) not in moved:
                        moved[g, m] = pltpu.roll(weights[g, at, :], L - m, 1)
                    return moved[g, m]

                for n in range(U * D):
                    total = None
                    for g in range(NSEG):
                        m, f = table[g][1][h * U * D + n]
                        term = (1.0 - f) * shifted(g, m) + f * shifted(g, m - 1)
                        total = term if total is None else total + term
                    back[k, n // D, n % D, at, :] = total

        by_half(act)
        image[rows_of(k, me), :] = back[k, unit, side]

    def returning(k):
        for r in range(U):
            to_unit = lax.rem(unit + r, U)
            for e in range(2):
                if r or e:
                    to_side = (side + e) % 2
                    i = 2 * r + e
                    yield remote(back.at[k, to_unit, to_side], image.at[rows_of(k, me), :], sem_b.at[k, i], sem_br.at[k, i],
                                 2 * to_side + flip, upper * U + to_unit)

    def finish(k):
        back_project(k)
        for copy in returning(k):
            copy.start()

    def arrive(k):
        for r in range(U):
            from_unit = lax.rem(unit + U - r, U)
            for e in range(2):
                if r or e:
                    from_side = (side + e) % 2
                    i = 2 * r + e
                    g = group(from_side, from_unit)
                    copy = remote(back.at[k, unit, side], image.at[rows_of(k, g), :], sem_b.at[k, i], sem_br.at[k, i],
                                  2 * from_side + flip, upper * U + from_unit)
                    guarded(k, g, copy.wait_recv)

    bands = square // LANES
    split = square - LANES
    regions = (
        ((0, half, 0, split, 0), (0, half, split, square, 1)),
        ((half, split, 0, split, 0), (half, split, split, square, 1), (split, 2 * half, 0, square, 1)),
    )
    shared = [min((a + 1) * LANES, half) - a * LANES for a in range(bands) if a * LANES < half]

    def swap(f, a):
        if f == 0:
            lanes = slice(a * LANES, (a + 1) * LANES)
            return remote(part.at[half:2 * half, lanes], other.at[:, lanes], sem_s.at[a], sem_sr.at[a], beside, slab)
        at = slice(a * LANES, a * LANES + shared[a])
        return remote(image.at[at, 0:square], other.at[at, :], sem_s.at[a], sem_sr.at[a], beside, slab)

    def spread(f, i, a_side, sems, to_view):
        r0, r1, l0, l1, _ = regions[f][i]
        place = whole.at[a_side, r0:r1, l0:l1]
        return remote(place, place, sems[0].at[i], sems[1].at[i], to_view, slab)

    def write(f, i, a_side, n):
        r0, r1, l0, l1, _ = regions[f][i]
        return pltpu.make_async_copy(whole.at[a_side, r0:r1, l0:l1], out_ref.at[r0:r1, a_side, l0:l1], sem_w.at[n, i])

    far_sems, near_sems, last_sems = (sem_f, sem_fr), (sem_n, sem_nr), (sem_t, sem_tr)

    def band(f, a):
        if f == 0:
            for b in range(0, square, LANES):
                part[b:b + LANES, a * LANES:(a + 1) * LANES] = image[a * LANES:(a + 1) * LANES, b:b + LANES].T
            swap(0, a).start()
        elif a < len(shared):
            swap(1, a).start()
        if a < bands - 2:
            return
        stage = a - (bands - 2)
        if f == 1:
            for n in range(bands - 1) if stage == 0 else (bands - 1,):
                swap(0, n).wait_recv()
        elif stage == 0:
            for n in range(len(shared)):
                swap(1, n).wait_recv()
        for i, (r0, r1, l0, l1, when) in enumerate(regions[f]):
            if when == stage:
                own = part if f == 0 else image
                whole[side, r0:r1, l0:l1] = own[r0:r1, l0:l1] + other[r0 - f * half:r1 - f * half, l0:l1]
                spread(f, i, side, far_sems, across).start()
                spread(f, i, side, near_sems, beside).start()
                write(f, i, side, 0).start()

    def settle(f):
        for i in range(len(regions[f])):
            spread(f, i, 1 - side, far_sems, across).wait_recv()
            spread(f, i, 1 - side, last_sems, beside).start()
            write(f, i, 1 - side, 1).start()
        for i in range(len(regions[1 - f])):
            spread(1 - f, i, side, near_sems, beside).wait_recv()
            write(1 - f, i, side, 2).start()
        for i in range(len(regions[1 - f])):
            spread(1 - f, i, 1 - side, last_sems, beside).wait_recv()
            write(1 - f, i, 1 - side, 3).start()
        for i in range(len(regions[f])):
            write(f, i, side, 0).wait()
            write(f, i, 1 - side, 1).wait()
        for i in range(len(regions[1 - f])):
            write(1 - f, i, side, 2).wait()
            write(1 - f, i, 1 - side, 3).wait()
        for a in range(bands if f == 0 else len(shared)):
            swap(f, a).wait_send()
        for i in range(len(regions[f])):
            spread(f, i, side, far_sems, across).wait_send()
            spread(f, i, side, near_sems, beside).wait_send()
            spread(f, i, 1 - side, last_sems, beside).wait_send()

    progress = {"arrived": 0, "band": 0}

    def ready(k):
        def act(n, carry):
            arrive(n)
            return carry

        lax.fori_loop(progress["arrived"], k + 1, act, 0)
        progress["arrived"] = k + 1
        while progress["band"] < bands and (k == K - 1 or (progress["band"] + 1) * LANES <= (k + 1) * G * CHUNK):
            for f in range(2):
                pl.when(flip == f)(functools.partial(band, f, progress["band"]))
            progress["band"] += 1

    def step(k, carry):
        @pl.when((k < K) & (k * G + me < chunks))
        def _():
            project(k)
            mid(k).start()

        @pl.when(k == 0)
        def _():
            for r in range(1, 4):
                from_view = lax.rem(view + 4 - r, 4)
                remote(em.at[flip, me], em_in.at[from_view], sem_e.at[r], sem_er.at[r], from_view, slab).wait_recv()

        if K > 1:
            @pl.when(k == K)
            def _():
                ready(K - 2)

        @pl.when((k > 0) & ((k - 1) * G + me < chunks))
        def _():
            finish(k - 1)

        return carry

    lax.fori_loop(0, K + 1, step, 0)
    ready(K - 1)
    for f in range(2):
        pl.when(flip == f)(functools.partial(settle, f))

    def drain(k, carry):
        for r in range(1, U):
            g, copy = outgoing(k, r)
            guarded(k, g, copy.wait_send)

        @pl.when(k * G + me < chunks)
        def _():
            mid(k).wait_send()
            for copy in returning(k):
                copy.wait_send()

        return carry

    lax.fori_loop(0, K, drain, 0)
    for copy in em_sends:
        copy.wait_send()


def on_device(atten, view_segment, efficiency, live_mask):
    S = lax.axis_size("slab")
    D, N = atten.shape[0], atten.shape[1]
    R = efficiency.shape[1]
    assert lax.axis_size("view") == 4 and D == 2 and efficiency.shape[0] == 2 and S % 2 == 0
    L = round_up(max(R + 1, N + S * D + 3), LANES)
    square = round_up(N, LANES)
    U = S // 2
    G = 2 * U
    K = -(-N // (G * CHUNK))
    half = round_up(N, 2 * TILE) // 2
    dims = (S, D, N, R, L, K, square, half)
    f32 = jnp.float32
    dma = pltpu.SemaphoreType.DMA
    far = pl.BlockSpec(memory_space=pl.ANY)
    out = pl.pallas_call(
        functools.partial(kernel, dims),
        out_shape=jax.ShapeDtypeStruct((2 * half, D, square), f32),
        in_specs=[pl.BlockSpec(memory_space=pltpu.SMEM), far, far, far],
        out_specs=far,
        scratch_shapes=[
            pltpu.VMEM((D, N, N), f32),
            pltpu.VMEM((2, N, R), f32),
            pltpu.VMEM((2, N, R), jnp.int32),
            pltpu.VMEM((D, square, L), f32),
            pltpu.VMEM((G, max(K, -(-square // (G * CHUNK))), D, CHUNK, L), f32),
            pltpu.VMEM((2, G, K, CHUNK, L), f32),
            pltpu.VMEM((K, U, D, CHUNK, L), f32),
            pltpu.VMEM((4, K, CHUNK, L), f32),
            pltpu.VMEM((K, NSEG, CHUNK, L), f32),
            pltpu.VMEM((K, NSEG, CHUNK, L), f32),
            pltpu.VMEM((NSEG, CHUNK, L), f32),
            pltpu.VMEM((K, U, D, CHUNK, L), f32),
            pltpu.VMEM((max(K * G * CHUNK, square), L), f32),
            pltpu.VMEM((square, square), f32),
            pltpu.VMEM((half, square), f32),
            pltpu.VMEM((D, 2 * half, square), f32),
            dma((D + 4,)),
            dma((K, U)), dma((K, U)), dma((4,)), dma((4,)),
            dma((K,)), dma((K,)), dma((K, G)), dma((K, G)),
            dma((square // LANES,)), dma((square // LANES,)), *[dma((3,))] * 6, dma((4, 3)),
        ],
        compiler_params=pltpu.CompilerParams(collective_id=0, has_side_effects=True, vmem_limit_bytes=63 * 2**20),
    )(view_segment, jnp.transpose(atten, (1, 0, 2)), jnp.transpose(efficiency, (2, 0, 1)), jnp.transpose(live_mask, (2, 0, 1)))
    return jnp.transpose(out[:N, :, :N], (1, 0, 2))


def solution(mesh):
    in_specs = (P("slab", None, None), P("view"), P("view", None, None), P("view", None, None))
    out_specs = P("slab", None, None)
    return jax.shard_map(on_device, mesh=mesh, in_specs=in_specs, out_specs=out_specs, check_vma=False)
```

```python
import functools
import math

import jax
import jax.numpy as jnp
from jax import lax
from jax.experimental import pallas as pl
from jax.experimental.pallas import tpu as pltpu
from jax.sharding import PartitionSpec as P

NSEG = 4
TILE = 8
LANES = 128
CHUNK = 16


def round_up(value, unit):
    return -(-value // unit) * unit


def geometry(segment, total):
    angle = (45.0 + 12.0 * segment / (NSEG - 1)) * (math.pi / 180.0)
    slope = math.cos(angle) / math.sin(angle)
    taps = []
    for z in range(total):
        centre = slope * (z + 0.5) - (total + 2.0)
        lower = math.floor(centre)
        taps.append((-lower, centre - lower))
    return math.sqrt(1.0 + slope * slope), taps


def kernel(dims, seg_ref, att_ref, eff_ref, live_ref, out_ref, att_v, eff_v, live_v, nat, src, em, slabs_in, em_in, mid_out, mid_in,
           weights, back, image, part, other, whole, sem_l, sem_g, sem_a, sem_ar, sem_e, sem_er, sem_m, sem_mr, sem_b, sem_br,
           sem_s, sem_sr, sem_f, sem_fr, sem_n, sem_nr, sem_t, sem_tr, sem_w):
    S, D, N, R, L, K, square, half = dims
    U = S // 2
    G = 2 * U
    chunks = -(-N // CHUNK)
    view, slab = lax.axis_index("view"), lax.axis_index("slab")
    side, flip = view // 2, view % 2
    upper, unit = slab // U, slab % U
    f32 = jnp.float32

    def group(a_side, a_unit):
        return a_unit * 2 + a_side

    def rows_of(k, g):
        return pl.ds(pl.multiple_of((k * G + g) * CHUNK, CHUNK), CHUNK)

    def guarded(k, g, act):
        if isinstance(k, int) and (k + 1) * G <= chunks:
            act()
        else:
            pl.when(k * G + g < chunks)(act)

    def remote(source, target, send, recv, to_view, to_slab):
        return pltpu.make_async_remote_copy(
            src_ref=source, dst_ref=target, send_sem=send, recv_sem=recv,
            device_id=(to_view, to_slab), device_id_type=pl.DeviceIdType.MESH)

    me = group(side, unit)
    across = 2 * (1 - side) + flip
    beside = 2 * side + 1 - flip
    corner = 2 * (1 - side) + 1 - flip
    partner = (1 - upper) * U + unit

    def in_half(r):
        return upper * U + lax.rem(unit + r, U)

    loads = []
    for d in range(D):
        loads.append(pltpu.make_async_copy(att_ref.at[:, d, :], att_v.at[d], sem_l.at[d]))
        loads[-1].start()

    full = N // CHUNK

    def gains(v, a, k, start):
        at = pl.ds(start, CHUNK)
        return (pltpu.make_async_copy(eff_ref.at[at, v, :], eff_v.at[v, a, k], sem_g.at[0, v, a, k]),
                pltpu.make_async_copy(live_ref.at[at, v, :], live_v.at[v, a, k], sem_g.at[1, v, a, k]))

    def load_gains(k, carry):
        for a in range(2):
            c = k * G + group(a, unit)
            for v in range(2):
                @pl.when(c < full)
                def _():
                    for copy in gains(v, a, k, c * CHUNK):
                        copy.start()

                @pl.when(c >= full)
                def _():
                    for copy in gains(v, a, k, N - CHUNK):
                        copy.start()
        return carry

    barrier = pltpu.get_barrier_semaphore()
    greet = [(view, in_half(r)) for r in range(1, U)] + [(across, in_half(r)) for r in range(U)]
    greet += [(beside, slab), (corner, slab), (view, partner)]
    for to in greet:
        pl.semaphore_signal(barrier, inc=1, device_id=to, device_id_type=pl.DeviceIdType.MESH)

    def zero_rows(i, carry):
        nat[i // (square // TILE), pl.ds(pl.multiple_of(i % (square // TILE) * TILE, TILE), TILE), :] = jnp.zeros((TILE, L), f32)
        return carry

    lax.fori_loop(0, D * square // TILE, zero_rows, 0)
    if L > square:
        src[:, :, :, :, square:L] = jnp.zeros((*src.shape[:4], L - square), f32)
    if chunks * CHUNK < image.shape[0]:
        image[chunks * CHUNK:, :] = jnp.zeros((image.shape[0] - chunks * CHUNK, L), f32)
    for d in range(D):
        loads[d].wait()
    lax.fori_loop(0, K, load_gains, 0)
    for d in range(D):
        nat[d, 0:N, 0:N] = att_v[d]

    pl.semaphore_wait(barrier, len(greet))

    def outgoing(k, r):
        to_unit = lax.rem(unit + r, U)
        g = group(side, to_unit)
        return g, remote(src.at[g, k], slabs_in.at[k, unit], sem_a.at[k, r], sem_ar.at[k, r], view, upper * U + to_unit)

    per_band = LANES // CHUNK
    started = 0
    for b in range(0, square, LANES):
        first = b // CHUNK

        @pl.when(flip == 1)
        def _():
            def act(i, carry):
                c = first + i
                src[c % G, c // G] = nat[:, pl.ds(pl.multiple_of(c * CHUNK, CHUNK), CHUNK), :]
                return carry

            lax.fori_loop(0, per_band, act, 0)

        @pl.when(flip == 0)
        def _():
            def act(d, carry):
                for a in range(0, square, LANES):
                    turned = nat[d, a:a + LANES, b:b + LANES].T
                    for i in range(per_band):
                        c = first + i
                        src[c % G, c // G, d, :, a:a + LANES] = turned[i * CHUNK:(i + 1) * CHUNK, :]
                return carry

            lax.fori_loop(0, D, act, 0)

        while started < K and ((started + 1) * G * CHUNK <= b + LANES or b + LANES == square):
            k = started
            for r in range(1, U):
                g, copy = outgoing(k, r)
                guarded(k, g, copy.start)

            def keep_own(k=k):
                slabs_in[k, unit] = src[me, k]

            guarded(k, me, keep_own)
            started += 1

    lane = lax.broadcasted_iota(jnp.int32, (CHUNK, LANES), 1)
    clear = R // LANES * LANES

    def fill(k, carry):
        for a in range(2):
            c = k * G + group(a, unit)
            for v in range(2):
                for copy in gains(v, a, k, N - CHUNK):
                    copy.wait()
                for b in range(clear, L, LANES):
                    blank = jnp.where(lane == LANES - 1, seg_ref[v].astype(f32), 0.0) if b + LANES == L else jnp.zeros((CHUNK, LANES), f32)
                    em[v, a, k, :, b:b + LANES] = blank
                gain = eff_v[v, a, k] * live_v[v, a, k].astype(f32)

                @pl.when(c < full)
                def _():
                    em[v, a, k, :, 0:R] = gain

                if N % CHUNK:
                    @pl.when(c >= full)
                    def _():
                        em[v, a, k, 0:N % CHUNK, 0:R] = gain[CHUNK - N % CHUNK:, :]
        return carry

    lax.fori_loop(0, K, fill, 0)
    em_sends = []
    for r in range(1, 4):
        to_view = lax.rem(view + r, 4)
        em_sends.append(remote(em.at[to_view % 2, to_view // 2], em_in.at[view], sem_e.at[r], sem_er.at[r], to_view, slab))
        em_sends[-1].start()
    em_in[view] = em[flip, side]

    table = [geometry(g, S * D) for g in range(NSEG)]

    def tiles(act):
        def step(t, carry):
            act(pl.ds(pl.multiple_of(t * TILE, TILE), TILE))
            return carry

        if CHUNK == TILE:
            act(slice(0, TILE))
        else:
            lax.fori_loop(0, CHUNK // TILE, step, 0)

    def by_half(act):
        pl.when(upper == 0)(functools.partial(act, 0))
        pl.when(upper == 1)(functools.partial(act, 1))

    def project(k):
        for r in range(1, U):
            from_unit = lax.rem(unit + U - r, U)
            remote(src.at[me, k], slabs_in.at[k, from_unit], sem_a.at[k, r], sem_ar.at[k, r], view, upper * U + from_unit).wait_recv()

        def act(h):
            @tiles
            def _(at):
                for g in range(NSEG):
                    length, taps = table[g]
                    sums = {}
                    for n in range(U * D):
                        m, f = taps[h * U * D + n]
                        plane = slabs_in[k, n // D, n % D, at, :]
                        for shift, coef in ((m, 1.0 - f), (m - 1, f)):
                            term = (length * coef) * plane
                            sums[shift] = sums[shift] + term if shift in sums else term
                    ray = None
                    for shift, value in sums.items():
                        moved = pltpu.roll(value, shift, 1)
                        ray = moved if ray is None else ray + moved
                    mid_out[k, g, at, :] = ray

        by_half(act)

    def mid(k):
        return remote(mid_out.at[k], mid_in.at[k], sem_m.at[k], sem_mr.at[k], view, partner)

    def back_project(k):
        mid(k).wait_recv()
        @tiles
        def _(at):
            for g in range(NSEG):
                gain = jnp.zeros((TILE, L), f32)
                for j in range(4):
                    one = em_in[j, k, at, :]
                    gain = gain + jnp.where(one[:, L - 1:L] == float(g), one, 0.0)
                weights[g, at, :] = table[g][0] * (gain * jnp.exp(-(mid_out[k, g, at, :] + mid_in[k, g, at, :])))

        def act(h):
            @tiles
            def _(at):
                moved = {}

                def shifted(g, m):
                    if (g, m) not in moved:
                        moved[g, m] = pltpu.roll(weights[g, at, :], L - m, 1)
                    return moved[g, m]

                for n in range(U * D):
                    total = None
                    for g in range(NSEG):
                        m, f = table[g][1][h * U * D + n]
                        term = (1.0 - f) * shifted(g, m) + f * shifted(g, m - 1)
                        total = term if total is None else total + term
                    back[k, n // D, n % D, at, :] = total

        by_half(act)
        image[rows_of(k, me), :] = back[k, unit, side]

    def returning(k):
        for r in range(U):
            to_unit = lax.rem(unit + r, U)
            for e in range(2):
                if r or e:
                    to_side = (side + e) % 2
                    i = 2 * r + e
                    yield remote(back.at[k, to_unit, to_side], image.at[rows_of(k, me), :], sem_b.at[k, i], sem_br.at[k, i],
                                 2 * to_side + flip, upper * U + to_unit)

    def finish(k):
        back_project(k)
        for copy in returning(k):
            copy.start()

    def arrive(k):
        for r in range(U):
            from_unit = lax.rem(unit + U - r, U)
            for e in range(2):
                if r or e:
                    from_side = (side + e) % 2
                    i = 2 * r + e
                    g = group(from_side, from_unit)
                    copy = remote(back.at[k, unit, side], image.at[rows_of(k, g), :], sem_b.at[k, i], sem_br.at[k, i],
                                  2 * from_side + flip, upper * U + from_unit)
                    guarded(k, g, copy.wait_recv)

    bands = square // LANES
    split = square - LANES
    regions = (
        ((0, half, 0, split, 0), (0, half, split, square, 1)),
        ((half, split, 0, split, 0), (half, split, split, square, 1), (split, 2 * half, 0, square, 1)),
    )
    shared = [min((a + 1) * LANES, half) - a * LANES for a in range(bands) if a * LANES < half]

    def swap(f, a):
        if f == 0:
            lanes = slice(a * LANES, (a + 1) * LANES)
            return remote(part.at[half:2 * half, lanes], other.at[:, lanes], sem_s.at[a], sem_sr.at[a], beside, slab)
        at = slice(a * LANES, a * LANES + shared[a])
        return remote(image.at[at, 0:square], other.at[at, :], sem_s.at[a], sem_sr.at[a], beside, slab)

    def spread(f, i, a_side, sems, to_view):
        r0, r1, l0, l1, _ = regions[f][i]
        place = whole.at[a_side, r0:r1, l0:l1]
        return remote(place, place, sems[0].at[i], sems[1].at[i], to_view, slab)

    def write(f, i, a_side, n):
        r0, r1, l0, l1, _ = regions[f][i]
        return pltpu.make_async_copy(whole.at[a_side, r0:r1, l0:l1], out_ref.at[r0:r1, a_side, l0:l1], sem_w.at[n, i])

    far_sems, near_sems, last_sems = (sem_f, sem_fr), (sem_n, sem_nr), (sem_t, sem_tr)

    def band(f, a):
        if f == 0:
            for b in range(0, square, LANES):
                part[b:b + LANES, a * LANES:(a + 1) * LANES] = image[a * LANES:(a + 1) * LANES, b:b + LANES].T
            swap(0, a).start()
        elif a < len(shared):
            swap(1, a).start()
        if a < bands - 2:
            return
        stage = a - (bands - 2)
        if f == 1:
            for n in range(bands - 1) if stage == 0 else (bands - 1,):
                swap(0, n).wait_recv()
        elif stage == 0:
            for n in range(len(shared)):
                swap(1, n).wait_recv()
        for i, (r0, r1, l0, l1, when) in enumerate(regions[f]):
            if when == stage:
                own = part if f == 0 else image
                whole[side, r0:r1, l0:l1] = own[r0:r1, l0:l1] + other[r0 - f * half:r1 - f * half, l0:l1]
                spread(f, i, side, far_sems, across).start()
                spread(f, i, side, near_sems, beside).start()
                write(f, i, side, 0).start()

    def settle(f):
        for i in range(len(regions[f])):
            spread(f, i, 1 - side, far_sems, across).wait_recv()
            spread(f, i, 1 - side, last_sems, beside).start()
            write(f, i, 1 - side, 1).start()
        for i in range(len(regions[1 - f])):
            spread(1 - f, i, side, near_sems, beside).wait_recv()
            write(1 - f, i, side, 2).start()
        for i in range(len(regions[1 - f])):
            spread(1 - f, i, 1 - side, last_sems, beside).wait_recv()
            write(1 - f, i, 1 - side, 3).start()
        for i in range(len(regions[f])):
            write(f, i, side, 0).wait()
            write(f, i, 1 - side, 1).wait()
        for i in range(len(regions[1 - f])):
            write(1 - f, i, side, 2).wait()
            write(1 - f, i, 1 - side, 3).wait()
        for a in range(bands if f == 0 else len(shared)):
            swap(f, a).wait_send()
        for i in range(len(regions[f])):
            spread(f, i, side, far_sems, across).wait_send()
            spread(f, i, side, near_sems, beside).wait_send()
            spread(f, i, 1 - side, last_sems, beside).wait_send()

    progress = {"arrived": 0, "band": 0}

    def ready(k):
        def act(n, carry):
            arrive(n)
            return carry

        lax.fori_loop(progress["arrived"], k + 1, act, 0)
        progress["arrived"] = k + 1
        while progress["band"] < bands and (k == K - 1 or (progress["band"] + 1) * LANES <= (k + 1) * G * CHUNK):
            for f in range(2):
                pl.when(flip == f)(functools.partial(band, f, progress["band"]))
            progress["band"] += 1

    def first_pass(k, carry):
        @pl.when(k * G + me < chunks)
        def _():
            project(k)
            mid(k).start()

        return carry

    lax.fori_loop(0, K, first_pass, 0)
    for r in range(1, 4):
        from_view = lax.rem(view + 4 - r, 4)
        remote(em.at[flip, side], em_in.at[from_view], sem_e.at[r], sem_er.at[r], from_view, slab).wait_recv()

    def second_pass(k, carry):
        if K > 1:
            @pl.when(k == K - 1)
            def _():
                ready(K - 2)

        @pl.when(k * G + me < chunks)
        def _():
            finish(k)

        return carry

    lax.fori_loop(0, K, second_pass, 0)
    ready(K - 1)
    for f in range(2):
        pl.when(flip == f)(functools.partial(settle, f))

    def drain(k, carry):
        for r in range(1, U):
            g, copy = outgoing(k, r)
            guarded(k, g, copy.wait_send)

        @pl.when(k * G + me < chunks)
        def _():
            mid(k).wait_send()
            for copy in returning(k):
                copy.wait_send()

        return carry

    lax.fori_loop(0, K, drain, 0)
    for copy in em_sends:
        copy.wait_send()


def on_device(atten, view_segment, efficiency, live_mask):
    S = lax.axis_size("slab")
    D, N = atten.shape[0], atten.shape[1]
    R = efficiency.shape[1]
    assert lax.axis_size("view") == 4 and D == 2 and efficiency.shape[0] == 2 and S % 2 == 0
    L = round_up(max(R + 1, N + S * D + 3), LANES)
    square = round_up(N, LANES)
    U = S // 2
    G = 2 * U
    K = -(-N // (G * CHUNK))
    half = round_up(N, 2 * TILE) // 2
    dims = (S, D, N, R, L, K, square, half)
    f32 = jnp.float32
    dma = pltpu.SemaphoreType.DMA
    far = pl.BlockSpec(memory_space=pl.ANY)
    out = pl.pallas_call(
        functools.partial(kernel, dims),
        out_shape=jax.ShapeDtypeStruct((2 * half, D, square), f32),
        in_specs=[pl.BlockSpec(memory_space=pltpu.SMEM), far, far, far],
        out_specs=far,
        scratch_shapes=[
            pltpu.VMEM((D, N, N), f32),
            pltpu.VMEM((2, 2, K, CHUNK, R), f32),
            pltpu.VMEM((2, 2, K, CHUNK, R), jnp.int32),
            pltpu.VMEM((D, square, L), f32),
            pltpu.VMEM((G, max(K, -(-square // (G * CHUNK))), D, CHUNK, L), f32),
            pltpu.VMEM((2, 2, K, CHUNK, L), f32),
            pltpu.VMEM((K, U, D, CHUNK, L), f32),
            pltpu.VMEM((4, K, CHUNK, L), f32),
            pltpu.VMEM((K, NSEG, CHUNK, L), f32),
            pltpu.VMEM((K, NSEG, CHUNK, L), f32),
            pltpu.VMEM((NSEG, CHUNK, L), f32),
            pltpu.VMEM((K, U, D, CHUNK, L), f32),
            pltpu.VMEM((max(K * G * CHUNK, square), L), f32),
            pltpu.VMEM((square, square), f32),
            pltpu.VMEM((half, square), f32),
            pltpu.VMEM((D, 2 * half, square), f32),
            dma((D,)), dma((2, 2, 2, K)),
            dma((K, U)), dma((K, U)), dma((4,)), dma((4,)),
            dma((K,)), dma((K,)), dma((K, G)), dma((K, G)),
            dma((square // LANES,)), dma((square // LANES,)), *[dma((3,))] * 6, dma((4, 3)),
        ],
        compiler_params=pltpu.CompilerParams(collective_id=0, has_side_effects=True, vmem_limit_bytes=63 * 2**20),
    )(view_segment, jnp.transpose(atten, (1, 0, 2)), jnp.transpose(efficiency, (2, 0, 1)), jnp.transpose(live_mask, (2, 0, 1)))
    return jnp.transpose(out[:N, :, :N], (1, 0, 2))


def solution(mesh):
    in_specs = (P("slab", None, None), P("view"), P("view", None, None), P("view", None, None))
    out_specs = P("slab", None, None)
    return jax.shard_map(on_device, mesh=mesh, in_specs=in_specs, out_specs=out_specs, check_vma=False)
```

```python
import functools
import math

import jax
import jax.numpy as jnp
from jax import lax
from jax.experimental import pallas as pl
from jax.experimental.pallas import tpu as pltpu
from jax.sharding import PartitionSpec as P

NSEG = 4
TILE = 8
LANES = 128
CHUNK = 8
AHEAD = 2


def round_up(value, unit):
    return -(-value // unit) * unit


def geometry(segment, total):
    angle = (45.0 + 12.0 * segment / (NSEG - 1)) * (math.pi / 180.0)
    slope = math.cos(angle) / math.sin(angle)
    taps = []
    for z in range(total):
        centre = slope * (z + 0.5) - (total + 2.0)
        lower = math.floor(centre)
        taps.append((-lower, centre - lower))
    return math.sqrt(1.0 + slope * slope), taps


def kernel(dims, seg_ref, att_ref, eff_ref, live_ref, out_ref, att_v, eff_v, live_v, nat, src, em, slabs_in, em_in, mid_out, mid_in,
           weights, back, image, part, other, whole, sem_l, sem_g, sem_a, sem_ar, sem_e, sem_er, sem_m, sem_mr, sem_b, sem_br,
           sem_s, sem_sr, sem_f, sem_fr, sem_n, sem_nr, sem_t, sem_tr, sem_w):
    S, D, N, R, L, K, square, half = dims
    U = S // 2
    G = 2 * U
    chunks = -(-N // CHUNK)
    view, slab = lax.axis_index("view"), lax.axis_index("slab")
    side, flip = view // 2, view % 2
    upper, unit = slab // U, slab % U
    f32 = jnp.float32

    def group(a_side, a_unit):
        return a_unit * 2 + a_side

    def rows_of(k, g):
        return pl.ds(pl.multiple_of((k * G + g) * CHUNK, CHUNK), CHUNK)

    def guarded(k, g, act):
        if isinstance(k, int) and (k + 1) * G <= chunks:
            act()
        else:
            pl.when(k * G + g < chunks)(act)

    def remote(source, target, send, recv, to_view, to_slab):
        return pltpu.make_async_remote_copy(
            src_ref=source, dst_ref=target, send_sem=send, recv_sem=recv,
            device_id=(to_view, to_slab), device_id_type=pl.DeviceIdType.MESH)

    me = group(side, unit)
    across = 2 * (1 - side) + flip
    beside = 2 * side + 1 - flip
    corner = 2 * (1 - side) + 1 - flip
    partner = (1 - upper) * U + unit

    def in_half(r):
        return upper * U + lax.rem(unit + r, U)

    loads = []
    for d in range(D):
        loads.append(pltpu.make_async_copy(att_ref.at[:, d, :], att_v.at[d], sem_l.at[d]))
        loads[-1].start()

    full = N // CHUNK

    def gains(v, a, k, start):
        at = pl.ds(start, CHUNK)
        return (pltpu.make_async_copy(eff_ref.at[at, v, :], eff_v.at[v, a, k], sem_g.at[0, v, a, k]),
                pltpu.make_async_copy(live_ref.at[at, v, :], live_v.at[v, a, k], sem_g.at[1, v, a, k]))

    def load_gains(k, carry):
        for a in range(2):
            c = k * G + group(a, unit)
            for v in range(2):
                @pl.when(c < full)
                def _():
                    for copy in gains(v, a, k, c * CHUNK):
                        copy.start()

                @pl.when(c >= full)
                def _():
                    for copy in gains(v, a, k, N - CHUNK):
                        copy.start()
        return carry

    barrier = pltpu.get_barrier_semaphore()
    greet = [(view, in_half(r)) for r in range(1, U)] + [(across, in_half(r)) for r in range(U)]
    greet += [(beside, slab), (corner, slab), (view, partner)]
    for to in greet:
        pl.semaphore_signal(barrier, inc=1, device_id=to, device_id_type=pl.DeviceIdType.MESH)

    def zero_rows(i, carry):
        nat[i // (square // TILE), pl.ds(pl.multiple_of(i % (square // TILE) * TILE, TILE), TILE), :] = jnp.zeros((TILE, L), f32)
        return carry

    lax.fori_loop(0, D * square // TILE, zero_rows, 0)
    if L > square:
        src[:, :, :, :, square:L] = jnp.zeros((*src.shape[:4], L - square), f32)
    if chunks * CHUNK < image.shape[0]:
        image[chunks * CHUNK:, :] = jnp.zeros((image.shape[0] - chunks * CHUNK, L), f32)
    for d in range(D):
        loads[d].wait()
    lax.fori_loop(0, K, load_gains, 0)
    for d in range(D):
        nat[d, 0:N, 0:N] = att_v[d]

    pl.semaphore_wait(barrier, len(greet))

    def outgoing(k, r):
        to_unit = lax.rem(unit + r, U)
        g = group(side, to_unit)
        return g, remote(src.at[g, k], slabs_in.at[k, unit], sem_a.at[k, r], sem_ar.at[k, r], view, upper * U + to_unit)

    per_band = LANES // CHUNK
    started = 0
    for b in range(0, square, LANES):
        first = b // CHUNK

        @pl.when(flip == 1)
        def _():
            def act(i, carry):
                c = first + i
                src[c % G, c // G] = nat[:, pl.ds(pl.multiple_of(c * CHUNK, CHUNK), CHUNK), :]
                return carry

            lax.fori_loop(0, per_band, act, 0)

        @pl.when(flip == 0)
        def _():
            def act(d, carry):
                for a in range(0, square, LANES):
                    turned = nat[d, a:a + LANES, b:b + LANES].T
                    for i in range(per_band):
                        c = first + i
                        src[c % G, c // G, d, :, a:a + LANES] = turned[i * CHUNK:(i + 1) * CHUNK, :]
                return carry

            lax.fori_loop(0, D, act, 0)

        while started < K and ((started + 1) * G * CHUNK <= b + LANES or b + LANES == square):
            k = started
            for r in range(1, U):
                g, copy = outgoing(k, r)
                guarded(k, g, copy.start)

            def keep_own(k=k):
                slabs_in[k, unit] = src[me, k]

            guarded(k, me, keep_own)
            started += 1

    lane = lax.broadcasted_iota(jnp.int32, (CHUNK, LANES), 1)
    clear = R // LANES * LANES

    def fill(k, carry):
        for a in range(2):
            c = k * G + group(a, unit)
            for v in range(2):
                for copy in gains(v, a, k, N - CHUNK):
                    copy.wait()
                for b in range(clear, L, LANES):
                    blank = jnp.where(lane == LANES - 1, seg_ref[v].astype(f32), 0.0) if b + LANES == L else jnp.zeros((CHUNK, LANES), f32)
                    em[v, a, k, :, b:b + LANES] = blank
                gain = eff_v[v, a, k] * live_v[v, a, k].astype(f32)

                @pl.when(c < full)
                def _():
                    em[v, a, k, :, 0:R] = gain

                if N % CHUNK:
                    @pl.when(c >= full)
                    def _():
                        em[v, a, k, 0:N % CHUNK, 0:R] = gain[CHUNK - N % CHUNK:, :]
        return carry

    lax.fori_loop(0, K, fill, 0)
    em_sends = []
    for r in range(1, 4):
        to_view = lax.rem(view + r, 4)
        em_sends.append(remote(em.at[to_view % 2, to_view // 2], em_in.at[view], sem_e.at[r], sem_er.at[r], to_view, slab))
        em_sends[-1].start()
    em_in[view] = em[flip, side]

    table = [geometry(g, S * D) for g in range(NSEG)]

    def tiles(act):
        def step(t, carry):
            act(pl.ds(pl.multiple_of(t * TILE, TILE), TILE))
            return carry

        if CHUNK == TILE:
            act(slice(0, TILE))
        else:
            lax.fori_loop(0, CHUNK // TILE, step, 0)

    def by_half(act):
        pl.when(upper == 0)(functools.partial(act, 0))
        pl.when(upper == 1)(functools.partial(act, 1))

    def project(k):
        for r in range(1, U):
            from_unit = lax.rem(unit + U - r, U)
            remote(src.at[me, k], slabs_in.at[k, from_unit], sem_a.at[k, r], sem_ar.at[k, r], view, upper * U + from_unit).wait_recv()

        def act(h):
            @tiles
            def _(at):
                for g in range(NSEG):
                    length, taps = table[g]
                    sums = {}
                    for n in range(U * D):
                        m, f = taps[h * U * D + n]
                        plane = slabs_in[k, n // D, n % D, at, :]
                        for shift, coef in ((m, 1.0 - f), (m - 1, f)):
                            term = (length * coef) * plane
                            sums[shift] = sums[shift] + term if shift in sums else term
                    ray = None
                    for shift, value in sums.items():
                        moved = pltpu.roll(value, shift, 1)
                        ray = moved if ray is None else ray + moved
                    mid_out[k, g, at, :] = ray

        by_half(act)

    def mid(k):
        return remote(mid_out.at[k], mid_in.at[k], sem_m.at[k], sem_mr.at[k], view, partner)

    def back_project(k):
        mid(k).wait_recv()
        @tiles
        def _(at):
            for g in range(NSEG):
                gain = jnp.zeros((TILE, L), f32)
                for j in range(4):
                    one = em_in[j, k, at, :]
                    gain = gain + jnp.where(one[:, L - 1:L] == float(g), one, 0.0)
                weights[g, at, :] = table[g][0] * (gain * jnp.exp(-(mid_out[k, g, at, :] + mid_in[k, g, at, :])))

        def act(h):
            @tiles
            def _(at):
                moved = {}

                def shifted(g, m):
                    if (g, m) not in moved:
                        moved[g, m] = pltpu.roll(weights[g, at, :], L - m, 1)
                    return moved[g, m]

                for n in range(U * D):
                    total = None
                    for g in range(NSEG):
                        m, f = table[g][1][h * U * D + n]
                        term = (1.0 - f) * shifted(g, m) + f * shifted(g, m - 1)
                        total = term if total is None else total + term
                    back[k, n // D, n % D, at, :] = total

        by_half(act)
        image[rows_of(k, me), :] = back[k, unit, side]

    def returning(k):
        for r in range(U):
            to_unit = lax.rem(unit + r, U)
            for e in range(2):
                if r or e:
                    to_side = (side + e) % 2
                    i = 2 * r + e
                    yield remote(back.at[k, to_unit, to_side], image.at[rows_of(k, me), :], sem_b.at[k, i], sem_br.at[k, i],
                                 2 * to_side + flip, upper * U + to_unit)

    def finish(k):
        back_project(k)
        for copy in returning(k):
            copy.start()

    def arrive(k):
        for r in range(U):
            from_unit = lax.rem(unit + U - r, U)
            for e in range(2):
                if r or e:
                    from_side = (side + e) % 2
                    i = 2 * r + e
                    g = group(from_side, from_unit)
                    copy = remote(back.at[k, unit, side], image.at[rows_of(k, g), :], sem_b.at[k, i], sem_br.at[k, i],
                                  2 * from_side + flip, upper * U + from_unit)
                    guarded(k, g, copy.wait_recv)

    bands = square // LANES
    split = square - LANES
    regions = (
        ((0, half, 0, split, 0), (0, half, split, square, 1)),
        ((half, split, 0, split, 0), (half, split, split, square, 1), (split, 2 * half, 0, square, 1)),
    )
    shared = [min((a + 1) * LANES, half) - a * LANES for a in range(bands) if a * LANES < half]

    def swap(f, a):
        if f == 0:
            lanes = slice(a * LANES, (a + 1) * LANES)
            return remote(part.at[half:2 * half, lanes], other.at[:, lanes], sem_s.at[a], sem_sr.at[a], beside, slab)
        at = slice(a * LANES, a * LANES + shared[a])
        return remote(image.at[at, 0:square], other.at[at, :], sem_s.at[a], sem_sr.at[a], beside, slab)

    def spread(f, i, a_side, sems, to_view):
        r0, r1, l0, l1, _ = regions[f][i]
        place = whole.at[a_side, r0:r1, l0:l1]
        return remote(place, place, sems[0].at[i], sems[1].at[i], to_view, slab)

    def write(f, i, a_side, n):
        r0, r1, l0, l1, _ = regions[f][i]
        return pltpu.make_async_copy(whole.at[a_side, r0:r1, l0:l1], out_ref.at[r0:r1, a_side, l0:l1], sem_w.at[n, i])

    far_sems, near_sems, last_sems = (sem_f, sem_fr), (sem_n, sem_nr), (sem_t, sem_tr)

    def band(f, a):
        if f == 0:
            for b in range(0, square, LANES):
                part[b:b + LANES, a * LANES:(a + 1) * LANES] = image[a * LANES:(a + 1) * LANES, b:b + LANES].T
            swap(0, a).start()
        elif a < len(shared):
            swap(1, a).start()
        if a < bands - 2:
            return
        stage = a - (bands - 2)
        if f == 1:
            for n in range(bands - 1) if stage == 0 else (bands - 1,):
                swap(0, n).wait_recv()
        elif stage == 0:
            for n in range(len(shared)):
                swap(1, n).wait_recv()
        for i, (r0, r1, l0, l1, when) in enumerate(regions[f]):
            if when == stage:
                own = part if f == 0 else image
                whole[side, r0:r1, l0:l1] = own[r0:r1, l0:l1] + other[r0 - f * half:r1 - f * half, l0:l1]
                spread(f, i, side, far_sems, across).start()
                spread(f, i, side, near_sems, beside).start()
                write(f, i, side, 0).start()

    def settle(f):
        for i in range(len(regions[f])):
            spread(f, i, 1 - side, far_sems, across).wait_recv()
            spread(f, i, 1 - side, last_sems, beside).start()
            write(f, i, 1 - side, 1).start()
        for i in range(len(regions[1 - f])):
            spread(1 - f, i, side, near_sems, beside).wait_recv()
            write(1 - f, i, side, 2).start()
        for i in range(len(regions[1 - f])):
            spread(1 - f, i, 1 - side, last_sems, beside).wait_recv()
            write(1 - f, i, 1 - side, 3).start()
        for i in range(len(regions[f])):
            write(f, i, side, 0).wait()
            write(f, i, 1 - side, 1).wait()
        for i in range(len(regions[1 - f])):
            write(1 - f, i, side, 2).wait()
            write(1 - f, i, 1 - side, 3).wait()
        for a in range(bands if f == 0 else len(shared)):
            swap(f, a).wait_send()
        for i in range(len(regions[f])):
            spread(f, i, side, far_sems, across).wait_send()
            spread(f, i, side, near_sems, beside).wait_send()
            spread(f, i, 1 - side, last_sems, beside).wait_send()

    progress = {"arrived": 0, "band": 0}

    def ready(k):
        def act(n, carry):
            arrive(n)
            return carry

        lax.fori_loop(progress["arrived"], k + 1, act, 0)
        progress["arrived"] = k + 1
        while progress["band"] < bands and (k == K - 1 or (progress["band"] + 1) * LANES <= (k + 1) * G * CHUNK):
            for f in range(2):
                pl.when(flip == f)(functools.partial(band, f, progress["band"]))
            progress["band"] += 1

    def step(k, carry):
        @pl.when((k < K) & (k * G + me < chunks))
        def _():
            project(k)
            mid(k).start()

        @pl.when(k == AHEAD)
        def _():
            for r in range(1, 4):
                from_view = lax.rem(view + 4 - r, 4)
                remote(em.at[flip, side], em_in.at[from_view], sem_e.at[r], sem_er.at[r], from_view, slab).wait_recv()

        if K > 1:
            @pl.when(k == K - 1 + AHEAD)
            def _():
                ready(K - 2)

        @pl.when((k >= AHEAD) & ((k - AHEAD) * G + me < chunks))
        def _():
            finish(k - AHEAD)

        return carry

    lax.fori_loop(0, K + AHEAD, step, 0)
    ready(K - 1)
    for f in range(2):
        pl.when(flip == f)(functools.partial(settle, f))

    def drain(k, carry):
        for r in range(1, U):
            g, copy = outgoing(k, r)
            guarded(k, g, copy.wait_send)

        @pl.when(k * G + me < chunks)
        def _():
            mid(k).wait_send()
            for copy in returning(k):
                copy.wait_send()

        return carry

    lax.fori_loop(0, K, drain, 0)
    for copy in em_sends:
        copy.wait_send()


def on_device(atten, view_segment, efficiency, live_mask):
    S = lax.axis_size("slab")
    D, N = atten.shape[0], atten.shape[1]
    R = efficiency.shape[1]
    assert lax.axis_size("view") == 4 and D == 2 and efficiency.shape[0] == 2 and S % 2 == 0
    L = round_up(max(R + 1, N + S * D + 3), LANES)
    square = round_up(N, LANES)
    U = S // 2
    G = 2 * U
    K = -(-N // (G * CHUNK))
    half = round_up(N, 2 * TILE) // 2
    dims = (S, D, N, R, L, K, square, half)
    f32 = jnp.float32
    dma = pltpu.SemaphoreType.DMA
    far = pl.BlockSpec(memory_space=pl.ANY)
    out = pl.pallas_call(
        functools.partial(kernel, dims),
        out_shape=jax.ShapeDtypeStruct((2 * half, D, square), f32),
        in_specs=[pl.BlockSpec(memory_space=pltpu.SMEM), far, far, far],
        out_specs=far,
        scratch_shapes=[
            pltpu.VMEM((D, N, N), f32),
            pltpu.VMEM((2, 2, K, CHUNK, R), f32),
            pltpu.VMEM((2, 2, K, CHUNK, R), jnp.int32),
            pltpu.VMEM((D, square, L), f32),
            pltpu.VMEM((G, max(K, -(-square // (G * CHUNK))), D, CHUNK, L), f32),
            pltpu.VMEM((2, 2, K, CHUNK, L), f32),
            pltpu.VMEM((K, U, D, CHUNK, L), f32),
            pltpu.VMEM((4, K, CHUNK, L), f32),
            pltpu.VMEM((K, NSEG, CHUNK, L), f32),
            pltpu.VMEM((K, NSEG, CHUNK, L), f32),
            pltpu.VMEM((NSEG, CHUNK, L), f32),
            pltpu.VMEM((K, U, D, CHUNK, L), f32),
            pltpu.VMEM((max(K * G * CHUNK, square), L), f32),
            pltpu.VMEM((square, square), f32),
            pltpu.VMEM((half, square), f32),
            pltpu.VMEM((D, 2 * half, square), f32),
            dma((D,)), dma((2, 2, 2, K)),
            dma((K, U)), dma((K, U)), dma((4,)), dma((4,)),
            dma((K,)), dma((K,)), dma((K, G)), dma((K, G)),
            dma((square // LANES,)), dma((square // LANES,)), *[dma((3,))] * 6, dma((4, 3)),
        ],
        compiler_params=pltpu.CompilerParams(collective_id=0, has_side_effects=True, vmem_limit_bytes=63 * 2**20),
    )(view_segment, jnp.transpose(atten, (1, 0, 2)), jnp.transpose(efficiency, (2, 0, 1)), jnp.transpose(live_mask, (2, 0, 1)))
    return jnp.transpose(out[:N, :, :N], (1, 0, 2))


def solution(mesh):
    in_specs = (P("slab", None, None), P("view"), P("view", None, None), P("view", None, None))
    out_specs = P("slab", None, None)
    return jax.shard_map(on_device, mesh=mesh, in_specs=in_specs, out_specs=out_specs, check_vma=False)
```

```python
import functools
import math

import jax
import jax.numpy as jnp
from jax import lax
from jax.experimental import pallas as pl
from jax.experimental.pallas import tpu as pltpu
from jax.sharding import PartitionSpec as P

NSEG = 4
TILE = 8
LANES = 128
CHUNK = 8
AHEAD = 2


def round_up(value, unit):
    return -(-value // unit) * unit


def geometry(segment, total):
    angle = (45.0 + 12.0 * segment / (NSEG - 1)) * (math.pi / 180.0)
    slope = math.cos(angle) / math.sin(angle)
    taps = []
    for z in range(total):
        centre = slope * (z + 0.5) - (total + 2.0)
        lower = math.floor(centre)
        taps.append((-lower, centre - lower))
    return math.sqrt(1.0 + slope * slope), taps


def kernel(dims, seg_ref, att_ref, eff_ref, live_ref, out_ref, att_v, eff_v, live_v, nat, src, em, slabs_in, em_in, mid_out, mid_in,
           weights, back, image, part, other, whole, sem_l, sem_g, sem_a, sem_ar, sem_e, sem_er, sem_m, sem_mr, sem_b, sem_br,
           sem_s, sem_sr, sem_f, sem_fr, sem_n, sem_nr, sem_t, sem_tr, sem_w):
    S, D, N, R, L, K, square, half = dims
    U = S // 2
    G = 2 * U
    chunks = -(-N // CHUNK)
    view, slab = lax.axis_index("view"), lax.axis_index("slab")
    side, flip = view // 2, view % 2
    upper, unit = slab // U, slab % U
    f32 = jnp.float32

    def group(a_side, a_unit):
        return a_unit * 2 + a_side

    def rows_of(k, g):
        return pl.ds(pl.multiple_of((k * G + g) * CHUNK, CHUNK), CHUNK)

    def guarded(k, g, act):
        if isinstance(k, int) and (k + 1) * G <= chunks:
            act()
        else:
            pl.when(k * G + g < chunks)(act)

    def remote(source, target, send, recv, to_view, to_slab):
        return pltpu.make_async_remote_copy(
            src_ref=source, dst_ref=target, send_sem=send, recv_sem=recv,
            device_id=(to_view, to_slab), device_id_type=pl.DeviceIdType.MESH)

    me = group(side, unit)
    across = 2 * (1 - side) + flip
    beside = 2 * side + 1 - flip
    corner = 2 * (1 - side) + 1 - flip
    partner = (1 - upper) * U + unit

    def in_half(r):
        return upper * U + lax.rem(unit + r, U)

    loads = []
    for d in range(D):
        loads.append(pltpu.make_async_copy(att_ref.at[:, d, :], att_v.at[d], sem_l.at[d]))
        loads[-1].start()

    full = N // CHUNK

    def gains(v, a, k, start):
        at = pl.ds(start, CHUNK)
        return (pltpu.make_async_copy(eff_ref.at[at, v, :], eff_v.at[v, a, k], sem_g.at[0, v, a, k]),
                pltpu.make_async_copy(live_ref.at[at, v, :], live_v.at[v, a, k], sem_g.at[1, v, a, k]))

    def load_gains(k, carry):
        for a in range(2):
            c = k * G + group(a, unit)
            for v in range(2):
                @pl.when(c < full)
                def _():
                    for copy in gains(v, a, k, c * CHUNK):
                        copy.start()

                @pl.when(c >= full)
                def _():
                    for copy in gains(v, a, k, N - CHUNK):
                        copy.start()
        return carry

    barrier = pltpu.get_barrier_semaphore()
    greet = [(view, in_half(r)) for r in range(1, U)] + [(across, in_half(r)) for r in range(U)]
    greet += [(beside, slab), (corner, slab), (view, partner)]
    for to in greet:
        pl.semaphore_signal(barrier, inc=1, device_id=to, device_id_type=pl.DeviceIdType.MESH)

    def zero_rows(i, carry):
        nat[i // (square // TILE), pl.ds(pl.multiple_of(i % (square // TILE) * TILE, TILE), TILE), :] = jnp.zeros((TILE, L), f32)
        return carry

    lax.fori_loop(0, D * square // TILE, zero_rows, 0)
    if L > square:
        src[:, :, :, :, square:L] = jnp.zeros((*src.shape[:4], L - square), f32)
    if chunks * CHUNK < image.shape[0]:
        image[chunks * CHUNK:, :] = jnp.zeros((image.shape[0] - chunks * CHUNK, L), f32)
    for d in range(D):
        loads[d].wait()
        if d == D - 1:
            lax.fori_loop(0, K, load_gains, 0)
        nat[d, 0:N, 0:N] = att_v[d]

    pl.semaphore_wait(barrier, len(greet))

    def outgoing(k, r):
        to_unit = lax.rem(unit + r, U)
        g = group(side, to_unit)
        return g, remote(src.at[g, k], slabs_in.at[k, unit], sem_a.at[k, r], sem_ar.at[k, r], view, upper * U + to_unit)

    per_band = LANES // CHUNK
    started = 0
    for b in range(0, square, LANES):
        first = b // CHUNK

        @pl.when(flip == 1)
        def _():
            def act(i, carry):
                c = first + i
                src[c % G, c // G] = nat[:, pl.ds(pl.multiple_of(c * CHUNK, CHUNK), CHUNK), :]
                return carry

            lax.fori_loop(0, per_band, act, 0)

        @pl.when(flip == 0)
        def _():
            def act(d, carry):
                for a in range(0, square, LANES):
                    turned = nat[d, a:a + LANES, b:b + LANES].T
                    for i in range(per_band):
                        c = first + i
                        src[c % G, c // G, d, :, a:a + LANES] = turned[i * CHUNK:(i + 1) * CHUNK, :]
                return carry

            lax.fori_loop(0, D, act, 0)

        while started < K and ((started + 1) * G * CHUNK <= b + LANES or b + LANES == square):
            k = started
            for r in range(1, U):
                g, copy = outgoing(k, r)
                guarded(k, g, copy.start)

            def keep_own(k=k):
                slabs_in[k, unit] = src[me, k]

            guarded(k, me, keep_own)
            started += 1

    lane = lax.broadcasted_iota(jnp.int32, (CHUNK, LANES), 1)
    clear = R // LANES * LANES

    def fill(k, carry):
        for a in range(2):
            c = k * G + group(a, unit)
            for v in range(2):
                for copy in gains(v, a, k, N - CHUNK):
                    copy.wait()
                for b in range(clear, L, LANES):
                    blank = jnp.where(lane == LANES - 1, seg_ref[v].astype(f32), 0.0) if b + LANES == L else jnp.zeros((CHUNK, LANES), f32)
                    em[v, a, k, :, b:b + LANES] = blank
                gain = eff_v[v, a, k] * live_v[v, a, k].astype(f32)

                @pl.when(c < full)
                def _():
                    em[v, a, k, :, 0:R] = gain

                if N % CHUNK:
                    @pl.when(c >= full)
                    def _():
                        em[v, a, k, 0:N % CHUNK, 0:R] = gain[CHUNK - N % CHUNK:, :]
        return carry

    lax.fori_loop(0, K, fill, 0)
    em_sends = []
    for r in range(1, 4):
        to_view = lax.rem(view + r, 4)
        em_sends.append(remote(em.at[to_view % 2, to_view // 2], em_in.at[view], sem_e.at[r], sem_er.at[r], to_view, slab))
        em_sends[-1].start()
    em_in[view] = em[flip, side]

    table = [geometry(g, S * D) for g in range(NSEG)]

    def tiles(act):
        def step(t, carry):
            act(pl.ds(pl.multiple_of(t * TILE, TILE), TILE))
            return carry

        if CHUNK == TILE:
            act(slice(0, TILE))
        else:
            lax.fori_loop(0, CHUNK // TILE, step, 0)

    def by_half(act):
        pl.when(upper == 0)(functools.partial(act, 0))
        pl.when(upper == 1)(functools.partial(act, 1))

    def project(k):
        for r in range(1, U):
            from_unit = lax.rem(unit + U - r, U)
            remote(src.at[me, k], slabs_in.at[k, from_unit], sem_a.at[k, r], sem_ar.at[k, r], view, upper * U + from_unit).wait_recv()

        def act(h):
            @tiles
            def _(at):
                for g in range(NSEG):
                    length, taps = table[g]
                    sums = {}
                    for n in range(U * D):
                        m, f = taps[h * U * D + n]
                        plane = slabs_in[k, n // D, n % D, at, :]
                        for shift, coef in ((m, 1.0 - f), (m - 1, f)):
                            term = (length * coef) * plane
                            sums[shift] = sums[shift] + term if shift in sums else term
                    ray = None
                    for shift, value in sums.items():
                        moved = pltpu.roll(value, shift, 1)
                        ray = moved if ray is None else ray + moved
                    mid_out[k, g, at, :] = ray

        by_half(act)

    def mid(k):
        return remote(mid_out.at[k], mid_in.at[k], sem_m.at[k], sem_mr.at[k], view, partner)

    def back_project(k):
        mid(k).wait_recv()
        @tiles
        def _(at):
            for g in range(NSEG):
                gain = jnp.zeros((TILE, L), f32)
                for j in range(4):
                    one = em_in[j, k, at, :]
                    gain = gain + jnp.where(one[:, L - 1:L] == float(g), one, 0.0)
                weights[g, at, :] = table[g][0] * (gain * jnp.exp(-(mid_out[k, g, at, :] + mid_in[k, g, at, :])))

        def act(h):
            @tiles
            def _(at):
                moved = {}

                def shifted(g, m):
                    if (g, m) not in moved:
                        moved[g, m] = pltpu.roll(weights[g, at, :], L - m, 1)
                    return moved[g, m]

                for n in range(U * D):
                    total = None
                    for g in range(NSEG):
                        m, f = table[g][1][h * U * D + n]
                        term = (1.0 - f) * shifted(g, m) + f * shifted(g, m - 1)
                        total = term if total is None else total + term
                    back[k, n // D, n % D, at, :] = total

        by_half(act)
        image[rows_of(k, me), :] = back[k, unit, side]

    def returning(k):
        for r in range(U):
            to_unit = lax.rem(unit + r, U)
            for e in range(2):
                if r or e:
                    to_side = (side + e) % 2
                    i = 2 * r + e
                    yield remote(back.at[k, to_unit, to_side], image.at[rows_of(k, me), :], sem_b.at[k, i], sem_br.at[k, i],
                                 2 * to_side + flip, upper * U + to_unit)

    def finish(k):
        back_project(k)
        for copy in returning(k):
            copy.start()

    def arrive(k):
        for r in range(U):
            from_unit = lax.rem(unit + U - r, U)
            for e in range(2):
                if r or e:
                    from_side = (side + e) % 2
                    i = 2 * r + e
                    g = group(from_side, from_unit)
                    copy = remote(back.at[k, unit, side], image.at[rows_of(k, g), :], sem_b.at[k, i], sem_br.at[k, i],
                                  2 * from_side + flip, upper * U + from_unit)
                    guarded(k, g, copy.wait_recv)

    bands = square // LANES
    split = square - LANES
    regions = (
        ((0, half, 0, split, 0), (0, half, split, square, 1)),
        ((half, split, 0, split, 0), (half, split, split, square, 1), (split, 2 * half, 0, square, 1)),
    )
    shared = [min((a + 1) * LANES, half) - a * LANES for a in range(bands) if a * LANES < half]

    def swap(f, a):
        if f == 0:
            lanes = slice(a * LANES, (a + 1) * LANES)
            return remote(part.at[half:2 * half, lanes], other.at[:, lanes], sem_s.at[a], sem_sr.at[a], beside, slab)
        at = slice(a * LANES, a * LANES + shared[a])
        return remote(image.at[at, 0:square], other.at[at, :], sem_s.at[a], sem_sr.at[a], beside, slab)

    def spread(f, i, a_side, sems, to_view):
        r0, r1, l0, l1, _ = regions[f][i]
        place = whole.at[a_side, r0:r1, l0:l1]
        return remote(place, place, sems[0].at[i], sems[1].at[i], to_view, slab)

    def write(f, i, a_side, n):
        r0, r1, l0, l1, _ = regions[f][i]
        return pltpu.make_async_copy(whole.at[a_side, r0:r1, l0:l1], out_ref.at[r0:r1, a_side, l0:l1], sem_w.at[n, i])

    far_sems, near_sems, last_sems = (sem_f, sem_fr), (sem_n, sem_nr), (sem_t, sem_tr)

    def band(f, a):
        if f == 0:
            for b in range(0, square, LANES):
                part[b:b + LANES, a * LANES:(a + 1) * LANES] = image[a * LANES:(a + 1) * LANES, b:b + LANES].T
            swap(0, a).start()
        elif a < len(shared):
            swap(1, a).start()
        if a < bands - 2:
            return
        stage = a - (bands - 2)
        if f == 1:
            for n in range(bands - 1) if stage == 0 else (bands - 1,):
                swap(0, n).wait_recv()
        elif stage == 0:
            for n in range(len(shared)):
                swap(1, n).wait_recv()
        for i, (r0, r1, l0, l1, when) in enumerate(regions[f]):
            if when == stage:
                own = part if f == 0 else image
                whole[side, r0:r1, l0:l1] = own[r0:r1, l0:l1] + other[r0 - f * half:r1 - f * half, l0:l1]
                spread(f, i, side, far_sems, across).start()
                spread(f, i, side, near_sems, beside).start()
                write(f, i, side, 0).start()

    def settle(f):
        for i in range(len(regions[f])):
            spread(f, i, 1 - side, far_sems, across).wait_recv()
            spread(f, i, 1 - side, last_sems, beside).start()
            write(f, i, 1 - side, 1).start()
        for i in range(len(regions[1 - f])):
            spread(1 - f, i, side, near_sems, beside).wait_recv()
            write(1 - f, i, side, 2).start()
        for a in range(bands if f == 0 else len(shared)):
            swap(f, a).wait_send()
        for i in range(len(regions[f])):
            spread(f, i, side, far_sems, across).wait_send()
            spread(f, i, side, near_sems, beside).wait_send()
            write(f, i, side, 0).wait()
        for i in range(len(regions[1 - f])):
            spread(1 - f, i, 1 - side, last_sems, beside).wait_recv()
            write(1 - f, i, 1 - side, 3).start()
        for i in range(len(regions[f])):
            spread(f, i, 1 - side, last_sems, beside).wait_send()
            write(f, i, 1 - side, 1).wait()
        for i in range(len(regions[1 - f])):
            write(1 - f, i, side, 2).wait()
            write(1 - f, i, 1 - side, 3).wait()

    progress = {"arrived": 0, "band": 0}

    def ready(k):
        def act(n, carry):
            arrive(n)
            return carry

        lax.fori_loop(progress["arrived"], k + 1, act, 0)
        progress["arrived"] = k + 1
        while progress["band"] < bands and (k == K - 1 or (progress["band"] + 1) * LANES <= (k + 1) * G * CHUNK):
            for f in range(2):
                pl.when(flip == f)(functools.partial(band, f, progress["band"]))
            progress["band"] += 1

    def step(k, carry):
        @pl.when((k < K) & (k * G + me < chunks))
        def _():
            project(k)
            mid(k).start()

        @pl.when(k == AHEAD)
        def _():
            for r in range(1, 4):
                from_view = lax.rem(view + 4 - r, 4)
                remote(em.at[flip, side], em_in.at[from_view], sem_e.at[r], sem_er.at[r], from_view, slab).wait_recv()

        if K > 1:
            @pl.when(k == K - 1 + AHEAD)
            def _():
                ready(K - 2)

        @pl.when((k >= AHEAD) & ((k - AHEAD) * G + me < chunks))
        def _():
            finish(k - AHEAD)

        return carry

    lax.fori_loop(0, K + AHEAD, step, 0)
    ready(K - 1)

    def drain(k, carry):
        for r in range(1, U):
            g, copy = outgoing(k, r)
            guarded(k, g, copy.wait_send)

        @pl.when(k * G + me < chunks)
        def _():
            mid(k).wait_send()
            for copy in returning(k):
                copy.wait_send()

        return carry

    lax.fori_loop(0, K, drain, 0)
    for copy in em_sends:
        copy.wait_send()
    for f in range(2):
        pl.when(flip == f)(functools.partial(settle, f))


def on_device(atten, view_segment, efficiency, live_mask):
    S = lax.axis_size("slab")
    D, N = atten.shape[0], atten.shape[1]
    R = efficiency.shape[1]
    assert lax.axis_size("view") == 4 and D == 2 and efficiency.shape[0] == 2 and S % 2 == 0
    L = round_up(max(R + 1, N + S * D + 3), LANES)
    square = round_up(N, LANES)
    U = S // 2
    G = 2 * U
    K = -(-N // (G * CHUNK))
    half = round_up(N, 2 * TILE) // 2
    dims = (S, D, N, R, L, K, square, half)
    f32 = jnp.float32
    dma = pltpu.SemaphoreType.DMA
    far = pl.BlockSpec(memory_space=pl.ANY)
    out = pl.pallas_call(
        functools.partial(kernel, dims),
        out_shape=pltpu.VMEM((2 * half, D, square), f32),
        in_specs=[pl.BlockSpec(memory_space=pltpu.SMEM), far, far, far],
        out_specs=pl.BlockSpec(memory_space=pltpu.VMEM),
        scratch_shapes=[
            pltpu.VMEM((D, N, N), f32),
            pltpu.VMEM((2, 2, K, CHUNK, R), f32),
            pltpu.VMEM((2, 2, K, CHUNK, R), jnp.int32),
            pltpu.VMEM((D, square, L), f32),
            pltpu.VMEM((G, max(K, -(-square // (G * CHUNK))), D, CHUNK, L), f32),
            pltpu.VMEM((2, 2, K, CHUNK, L), f32),
            pltpu.VMEM((K, U, D, CHUNK, L), f32),
            pltpu.VMEM((4, K, CHUNK, L), f32),
            pltpu.VMEM((K, NSEG, CHUNK, L), f32),
            pltpu.VMEM((K, NSEG, CHUNK, L), f32),
            pltpu.VMEM((NSEG, CHUNK, L), f32),
            pltpu.VMEM((K, U, D, CHUNK, L), f32),
            pltpu.VMEM((max(K * G * CHUNK, square), L), f32),
            pltpu.VMEM((square, square), f32),
            pltpu.VMEM((half, square), f32),
            pltpu.VMEM((D, 2 * half, square), f32),
            dma((D,)), dma((2, 2, 2, K)),
            dma((K, U)), dma((K, U)), dma((4,)), dma((4,)),
            dma((K,)), dma((K,)), dma((K, G)), dma((K, G)),
            dma((square // LANES,)), dma((square // LANES,)), *[dma((3,))] * 6, dma((4, 3)),
        ],
        compiler_params=pltpu.CompilerParams(collective_id=0, has_side_effects=True, vmem_limit_bytes=61 * 2**20),
    )(view_segment, jnp.transpose(atten, (1, 0, 2)), jnp.transpose(efficiency, (2, 0, 1)), jnp.transpose(live_mask, (2, 0, 1)))
    return jnp.transpose(out[:N, :, :N], (1, 0, 2))


def solution(mesh):
    in_specs = (P("slab", None, None), P("view"), P("view", None, None), P("view", None, None))
    out_specs = P("slab", None, None)
    return jax.shard_map(on_device, mesh=mesh, in_specs=in_specs, out_specs=out_specs, check_vma=False)
```

```python
import functools
import math

import jax
import jax.numpy as jnp
from jax import lax
from jax.experimental import pallas as pl
from jax.experimental.pallas import tpu as pltpu
from jax.sharding import PartitionSpec as P

NSEG = 4
TILE = 8
LANES = 128
CHUNK = 16
AHEAD = 1


def round_up(value, unit):
    return -(-value // unit) * unit


def geometry(segment, total):
    angle = (45.0 + 12.0 * segment / (NSEG - 1)) * (math.pi / 180.0)
    slope = math.cos(angle) / math.sin(angle)
    taps = []
    for z in range(total):
        centre = slope * (z + 0.5) - (total + 2.0)
        lower = math.floor(centre)
        taps.append((-lower, centre - lower))
    return math.sqrt(1.0 + slope * slope), taps


def kernel(dims, seg_ref, att_ref, eff_ref, live_ref, out_ref, att_v, eff_v, live_v, nat, src, em, slabs_in, em_in, mid_out, mid_in,
           weights, back, image, part, other, whole, sem_l, sem_g, sem_a, sem_ar, sem_e, sem_er, sem_m, sem_mr, sem_b, sem_br,
           sem_s, sem_sr, sem_f, sem_fr, sem_n, sem_nr, sem_t, sem_tr, sem_w):
    S, D, N, R, L, K, square, half = dims
    U = S // 2
    G = 2 * U
    chunks = -(-N // CHUNK)
    view, slab = lax.axis_index("view"), lax.axis_index("slab")
    side, flip = view // 2, view % 2
    upper, unit = slab // U, slab % U
    f32 = jnp.float32

    def group(a_side, a_unit):
        return a_unit * 2 + a_side

    def rows_of(k, g):
        return pl.ds(pl.multiple_of((k * G + g) * CHUNK, CHUNK), CHUNK)

    def guarded(k, g, act):
        if isinstance(k, int) and (k + 1) * G <= chunks:
            act()
        else:
            pl.when(k * G + g < chunks)(act)

    def remote(source, target, send, recv, to_view, to_slab):
        return pltpu.make_async_remote_copy(
            src_ref=source, dst_ref=target, send_sem=send, recv_sem=recv,
            device_id=(to_view, to_slab), device_id_type=pl.DeviceIdType.MESH)

    me = group(side, unit)
    across = 2 * (1 - side) + flip
    beside = 2 * side + 1 - flip
    corner = 2 * (1 - side) + 1 - flip
    partner = (1 - upper) * U + unit

    def in_half(r):
        return upper * U + lax.rem(unit + r, U)

    loads = []
    for d in range(D):
        loads.append(pltpu.make_async_copy(att_ref.at[:, d, :], att_v.at[d], sem_l.at[d]))
        loads[-1].start()

    full = N // CHUNK

    def gains(v, a, k, start):
        at = pl.ds(start, CHUNK)
        return (pltpu.make_async_copy(eff_ref.at[at, v, :], eff_v.at[v, a, k], sem_g.at[0, v, a, k]),
                pltpu.make_async_copy(live_ref.at[at, v, :], live_v.at[v, a, k], sem_g.at[1, v, a, k]))

    def load_gains(k, carry):
        for a in range(2):
            c = k * G + group(a, unit)
            for v in range(2):
                @pl.when(c < full)
                def _():
                    for copy in gains(v, a, k, c * CHUNK):
                        copy.start()

                @pl.when(c >= full)
                def _():
                    for copy in gains(v, a, k, N - CHUNK):
                        copy.start()
        return carry

    barrier = pltpu.get_barrier_semaphore()
    greet = [(view, in_half(r)) for r in range(1, U)] + [(across, in_half(r)) for r in range(U)]
    greet += [(beside, slab), (corner, slab), (view, partner)]
    for to in greet:
        pl.semaphore_signal(barrier, inc=1, device_id=to, device_id_type=pl.DeviceIdType.MESH)

    def zero_rows(i, carry):
        nat[i // (square // TILE), pl.ds(pl.multiple_of(i % (square // TILE) * TILE, TILE), TILE), :] = jnp.zeros((TILE, L), f32)
        return carry

    lax.fori_loop(0, D * square // TILE, zero_rows, 0)
    if L > square:
        src[:, :, :, :, square:L] = jnp.zeros((*src.shape[:4], L - square), f32)
    if chunks * CHUNK < image.shape[0]:
        image[chunks * CHUNK:, :] = jnp.zeros((image.shape[0] - chunks * CHUNK, L), f32)
    for d in range(D):
        loads[d].wait()
        if d == D - 1:
            lax.fori_loop(0, K, load_gains, 0)
        nat[d, 0:N, 0:N] = att_v[d]

    pl.semaphore_wait(barrier, len(greet))

    def outgoing(k, r):
        to_unit = lax.rem(unit + r, U)
        g = group(side, to_unit)
        return g, remote(src.at[g, k], slabs_in.at[k, unit], sem_a.at[k, r], sem_ar.at[k, r], view, upper * U + to_unit)

    per_band = LANES // CHUNK
    started = 0
    for b in range(0, square, LANES):
        first = b // CHUNK

        @pl.when(flip == 1)
        def _():
            def act(i, carry):
                c = first + i
                src[c % G, c // G] = nat[:, pl.ds(pl.multiple_of(c * CHUNK, CHUNK), CHUNK), :]
                return carry

            lax.fori_loop(0, per_band, act, 0)

        @pl.when(flip == 0)
        def _():
            def act(d, carry):
                for a in range(0, square, LANES):
                    turned = nat[d, a:a + LANES, b:b + LANES].T
                    for i in range(per_band):
                        c = first + i
                        src[c % G, c // G, d, :, a:a + LANES] = turned[i * CHUNK:(i + 1) * CHUNK, :]
                return carry

            lax.fori_loop(0, D, act, 0)

        while started < K and ((started + 1) * G * CHUNK <= b + LANES or b + LANES == square):
            k = started
            for r in range(1, U):
                g, copy = outgoing(k, r)
                guarded(k, g, copy.start)

            def keep_own(k=k):
                slabs_in[k, unit] = src[me, k]

            guarded(k, me, keep_own)
            started += 1

    lane = lax.broadcasted_iota(jnp.int32, (CHUNK, LANES), 1)
    clear = R // LANES * LANES

    def fill(k, carry):
        for a in range(2):
            c = k * G + group(a, unit)
            for v in range(2):
                for copy in gains(v, a, k, N - CHUNK):
                    copy.wait()
                for b in range(clear, L, LANES):
                    blank = jnp.where(lane == LANES - 1, seg_ref[v].astype(f32), 0.0) if b + LANES == L else jnp.zeros((CHUNK, LANES), f32)
                    em[v, a, k, :, b:b + LANES] = blank
                gain = eff_v[v, a, k] * live_v[v, a, k].astype(f32)

                @pl.when(c < full)
                def _():
                    em[v, a, k, :, 0:R] = gain

                if N % CHUNK:
                    @pl.when(c >= full)
                    def _():
                        em[v, a, k, 0:N % CHUNK, 0:R] = gain[CHUNK - N % CHUNK:, :]
        return carry

    lax.fori_loop(0, K, fill, 0)
    em_sends = []
    for r in range(1, 4):
        to_view = lax.rem(view + r, 4)
        em_sends.append(remote(em.at[to_view % 2, to_view // 2], em_in.at[view], sem_e.at[r], sem_er.at[r], to_view, slab))
        em_sends[-1].start()
    em_in[view] = em[flip, side]

    table = [geometry(g, S * D) for g in range(NSEG)]

    def tiles(act):
        def step(t, carry):
            act(pl.ds(pl.multiple_of(t * TILE, TILE), TILE))
            return carry

        if CHUNK == TILE:
            act(slice(0, TILE))
        else:
            lax.fori_loop(0, CHUNK // TILE, step, 0)

    def by_half(act):
        pl.when(upper == 0)(functools.partial(act, 0))
        pl.when(upper == 1)(functools.partial(act, 1))

    def project(k):
        for r in range(1, U):
            from_unit = lax.rem(unit + U - r, U)
            remote(src.at[me, k], slabs_in.at[k, from_unit], sem_a.at[k, r], sem_ar.at[k, r], view, upper * U + from_unit).wait_recv()

        def act(h):
            @tiles
            def _(at):
                for g in range(NSEG):
                    length, taps = table[g]
                    sums = {}
                    for n in range(U * D):
                        m, f = taps[h * U * D + n]
                        plane = slabs_in[k, n // D, n % D, at, :]
                        for shift, coef in ((m, 1.0 - f), (m - 1, f)):
                            term = (length * coef) * plane
                            sums[shift] = sums[shift] + term if shift in sums else term
                    ray = None
                    for shift, value in sums.items():
                        moved = pltpu.roll(value, shift, 1)
                        ray = moved if ray is None else ray + moved
                    mid_out[k, g, at, :] = ray

        by_half(act)

    def mid(k):
        return remote(mid_out.at[k], mid_in.at[k], sem_m.at[k], sem_mr.at[k], view, partner)

    def back_project(k):
        mid(k).wait_recv()
        @tiles
        def _(at):
            for g in range(NSEG):
                gain = jnp.zeros((TILE, L), f32)
                for j in range(4):
                    one = em_in[j, k, at, :]
                    gain = gain + jnp.where(one[:, L - 1:L] == float(g), one, 0.0)
                weights[g, at, :] = table[g][0] * (gain * jnp.exp(-(mid_out[k, g, at, :] + mid_in[k, g, at, :])))

        def act(h):
            @tiles
            def _(at):
                moved = {}

                def shifted(g, m):
                    if (g, m) not in moved:
                        moved[g, m] = pltpu.roll(weights[g, at, :], L - m, 1)
                    return moved[g, m]

                for n in range(U * D):
                    total = None
                    for g in range(NSEG):
                        m, f = table[g][1][h * U * D + n]
                        term = (1.0 - f) * shifted(g, m) + f * shifted(g, m - 1)
                        total = term if total is None else total + term
                    back[k, n // D, n % D, at, :] = total

        by_half(act)
        image[rows_of(k, me), :] = back[k, unit, side]

    def returning(k):
        for r in range(U):
            to_unit = lax.rem(unit + r, U)
            for e in range(2):
                if r or e:
                    to_side = (side + e) % 2
                    i = 2 * r + e
                    yield remote(back.at[k, to_unit, to_side], image.at[rows_of(k, me), :], sem_b.at[k, i], sem_br.at[k, i],
                                 2 * to_side + flip, upper * U + to_unit)

    def finish(k):
        back_project(k)
        for copy in returning(k):
            copy.start()

    def arrive(k):
        for r in range(U):
            from_unit = lax.rem(unit + U - r, U)
            for e in range(2):
                if r or e:
                    from_side = (side + e) % 2
                    i = 2 * r + e
                    g = group(from_side, from_unit)
                    copy = remote(back.at[k, unit, side], image.at[rows_of(k, g), :], sem_b.at[k, i], sem_br.at[k, i],
                                  2 * from_side + flip, upper * U + from_unit)
                    guarded(k, g, copy.wait_recv)

    bands = square // LANES
    split = square - LANES
    regions = (
        ((0, half, 0, split, 0), (0, half, split, square, 1)),
        ((half, split, 0, split, 0), (half, split, split, square, 1), (split, 2 * half, 0, square, 1)),
    )
    shared = [min((a + 1) * LANES, half) - a * LANES for a in range(bands) if a * LANES < half]

    def swap(f, a):
        if f == 0:
            lanes = slice(a * LANES, (a + 1) * LANES)
            return remote(part.at[half:2 * half, lanes], other.at[:, lanes], sem_s.at[a], sem_sr.at[a], beside, slab)
        at = slice(a * LANES, a * LANES + shared[a])
        return remote(image.at[at, 0:square], other.at[at, :], sem_s.at[a], sem_sr.at[a], beside, slab)

    def spread(f, i, a_side, sems, to_view):
        r0, r1, l0, l1, _ = regions[f][i]
        place = whole.at[a_side, r0:r1, l0:l1]
        return remote(place, place, sems[0].at[i], sems[1].at[i], to_view, slab)

    def write(f, i, a_side, n):
        r0, r1, l0, l1, _ = regions[f][i]
        return pltpu.make_async_copy(whole.at[a_side, r0:r1, l0:l1], out_ref.at[r0:r1, a_side, l0:l1], sem_w.at[n, i])

    far_sems, near_sems, last_sems = (sem_f, sem_fr), (sem_n, sem_nr), (sem_t, sem_tr)

    def band(f, a):
        if f == 0:
            for b in range(0, square, LANES):
                part[b:b + LANES, a * LANES:(a + 1) * LANES] = image[a * LANES:(a + 1) * LANES, b:b + LANES].T
            swap(0, a).start()
        elif a < len(shared):
            swap(1, a).start()
        if a < bands - 2:
            return
        stage = a - (bands - 2)
        if f == 1:
            for n in range(bands - 1) if stage == 0 else (bands - 1,):
                swap(0, n).wait_recv()
        elif stage == 0:
            for n in range(len(shared)):
                swap(1, n).wait_recv()
        for i, (r0, r1, l0, l1, when) in enumerate(regions[f]):
            if when == stage:
                own = part if f == 0 else image
                whole[side, r0:r1, l0:l1] = own[r0:r1, l0:l1] + other[r0 - f * half:r1 - f * half, l0:l1]
                spread(f, i, side, far_sems, across).start()
                spread(f, i, side, near_sems, beside).start()
                write(f, i, side, 0).start()

    def settle(f):
        for i in range(len(regions[f])):
            spread(f, i, 1 - side, far_sems, across).wait_recv()
            spread(f, i, 1 - side, last_sems, beside).start()
            write(f, i, 1 - side, 1).start()
        for i in range(len(regions[1 - f])):
            spread(1 - f, i, side, near_sems, beside).wait_recv()
            write(1 - f, i, side, 2).start()
        for a in range(bands if f == 0 else len(shared)):
            swap(f, a).wait_send()
        for i in range(len(regions[f])):
            spread(f, i, side, far_sems, across).wait_send()
            spread(f, i, side, near_sems, beside).wait_send()
            write(f, i, side, 0).wait()
        for i in range(len(regions[1 - f])):
            spread(1 - f, i, 1 - side, last_sems, beside).wait_recv()
            write(1 - f, i, 1 - side, 3).start()
        for i in range(len(regions[f])):
            spread(f, i, 1 - side, last_sems, beside).wait_send()
            write(f, i, 1 - side, 1).wait()
        for i in range(len(regions[1 - f])):
            write(1 - f, i, side, 2).wait()
            write(1 - f, i, 1 - side, 3).wait()

    progress = {"arrived": 0, "band": 0}

    def ready(k):
        def act(n, carry):
            arrive(n)
            return carry

        lax.fori_loop(progress["arrived"], k + 1, act, 0)
        progress["arrived"] = k + 1
        while progress["band"] < bands and (k == K - 1 or (progress["band"] + 1) * LANES <= (k + 1) * G * CHUNK):
            for f in range(2):
                pl.when(flip == f)(functools.partial(band, f, progress["band"]))
            progress["band"] += 1

    def step(k, carry):
        @pl.when((k < K) & (k * G + me < chunks))
        def _():
            project(k)
            mid(k).start()

        @pl.when(k == AHEAD)
        def _():
            for r in range(1, 4):
                from_view = lax.rem(view + 4 - r, 4)
                remote(em.at[flip, side], em_in.at[from_view], sem_e.at[r], sem_er.at[r], from_view, slab).wait_recv()

        if K > 1:
            @pl.when(k == K - 1 + AHEAD)
            def _():
                ready(K - 2)

        @pl.when((k >= AHEAD) & ((k - AHEAD) * G + me < chunks))
        def _():
            finish(k - AHEAD)

        return carry

    lax.fori_loop(0, K + AHEAD, step, 0)
    ready(K - 1)

    def drain(k, carry):
        for r in range(1, U):
            g, copy = outgoing(k, r)
            guarded(k, g, copy.wait_send)

        @pl.when(k * G + me < chunks)
        def _():
            mid(k).wait_send()
            for copy in returning(k):
                copy.wait_send()

        return carry

    lax.fori_loop(0, K, drain, 0)
    for copy in em_sends:
        copy.wait_send()
    for f in range(2):
        pl.when(flip == f)(functools.partial(settle, f))


def on_device(atten, view_segment, efficiency, live_mask):
    S = lax.axis_size("slab")
    D, N = atten.shape[0], atten.shape[1]
    R = efficiency.shape[1]
    assert lax.axis_size("view") == 4 and D == 2 and efficiency.shape[0] == 2 and S % 2 == 0
    L = round_up(max(R + 1, N + S * D + 3), LANES)
    square = round_up(N, LANES)
    U = S // 2
    G = 2 * U
    K = -(-N // (G * CHUNK))
    half = round_up(N, 2 * TILE) // 2
    dims = (S, D, N, R, L, K, square, half)
    f32 = jnp.float32
    dma = pltpu.SemaphoreType.DMA
    far = pl.BlockSpec(memory_space=pl.ANY)
    out = pl.pallas_call(
        functools.partial(kernel, dims),
        out_shape=pltpu.VMEM((2 * half, D, square), f32),
        in_specs=[pl.BlockSpec(memory_space=pltpu.SMEM), far, far, far],
        out_specs=pl.BlockSpec(memory_space=pltpu.VMEM),
        scratch_shapes=[
            pltpu.VMEM((D, N, N), f32),
            pltpu.VMEM((2, 2, K, CHUNK, R), f32),
            pltpu.VMEM((2, 2, K, CHUNK, R), jnp.int32),
            pltpu.VMEM((D, square, L), f32),
            pltpu.VMEM((G, max(K, -(-square // (G * CHUNK))), D, CHUNK, L), f32),
            pltpu.VMEM((2, 2, K, CHUNK, L), f32),
            pltpu.VMEM((K, U, D, CHUNK, L), f32),
            pltpu.VMEM((4, K, CHUNK, L), f32),
            pltpu.VMEM((K, NSEG, CHUNK, L), f32),
            pltpu.VMEM((K, NSEG, CHUNK, L), f32),
            pltpu.VMEM((NSEG, CHUNK, L), f32),
            pltpu.VMEM((K, U, D, CHUNK, L), f32),
            pltpu.VMEM((max(K * G * CHUNK, square), L), f32),
            pltpu.VMEM((square, square), f32),
            pltpu.VMEM((half, square), f32),
            pltpu.VMEM((D, 2 * half, square), f32),
            dma((D,)), dma((2, 2, 2, K)),
            dma((K, U)), dma((K, U)), dma((4,)), dma((4,)),
            dma((K,)), dma((K,)), dma((K, G)), dma((K, G)),
            dma((square // LANES,)), dma((square // LANES,)), *[dma((3,))] * 6, dma((4, 3)),
        ],
        compiler_params=pltpu.CompilerParams(collective_id=0, has_side_effects=True, vmem_limit_bytes=61 * 2**20),
    )(view_segment, jnp.transpose(atten, (1, 0, 2)), jnp.transpose(efficiency, (2, 0, 1)), jnp.transpose(live_mask, (2, 0, 1)))
    return jnp.transpose(out[:N, :, :N], (1, 0, 2))


def solution(mesh):
    in_specs = (P("slab", None, None), P("view"), P("view", None, None), P("view", None, None))
    out_specs = P("slab", None, None)
    return jax.shard_map(on_device, mesh=mesh, in_specs=in_specs, out_specs=out_specs, check_vma=False)
```

```python
import functools
import math

import jax
import jax.numpy as jnp
from jax import lax
from jax.experimental import pallas as pl
from jax.experimental.pallas import tpu as pltpu
from jax.sharding import PartitionSpec as P

NSEG = 4
TILE = 8
LANES = 128
CHUNK = 16
AHEAD = 1


def round_up(value, unit):
    return -(-value // unit) * unit


def geometry(segment, total):
    angle = (45.0 + 12.0 * segment / (NSEG - 1)) * (math.pi / 180.0)
    slope = math.cos(angle) / math.sin(angle)
    taps = []
    for z in range(total):
        centre = slope * (z + 0.5) - (total + 2.0)
        lower = math.floor(centre)
        taps.append((-lower, centre - lower))
    return math.sqrt(1.0 + slope * slope), taps


def kernel(dims, seg_ref, att_ref, eff_ref, live_ref, out_ref, att_v, eff_v, live_v, nat, src, em, slabs_in, em_in, mid_out, mid_in,
           weights, back, image, part, other, whole, sem_l, sem_g, sem_a, sem_ar, sem_e, sem_er, sem_m, sem_mr, sem_b, sem_br,
           sem_s, sem_sr, sem_f, sem_fr, sem_n, sem_nr, sem_t, sem_tr, sem_w):
    S, D, N, R, L, K, square, half = dims
    U = S // 2
    G = 2 * U
    chunks = -(-N // CHUNK)
    view, slab = lax.axis_index("view"), lax.axis_index("slab")
    side, flip = view // 2, view % 2
    upper, unit = slab // U, slab % U
    f32 = jnp.float32

    def group(a_side, a_unit):
        return a_unit * 2 + a_side

    def rows_of(k, g):
        return pl.ds(pl.multiple_of((k * G + g) * CHUNK, CHUNK), CHUNK)

    def guarded(k, g, act):
        if isinstance(k, int) and (k + 1) * G <= chunks:
            act()
        else:
            pl.when(k * G + g < chunks)(act)

    def remote(source, target, send, recv, to_view, to_slab):
        return pltpu.make_async_remote_copy(
            src_ref=source, dst_ref=target, send_sem=send, recv_sem=recv,
            device_id=(to_view, to_slab), device_id_type=pl.DeviceIdType.MESH)

    me = group(side, unit)
    across = 2 * (1 - side) + flip
    beside = 2 * side + 1 - flip
    corner = 2 * (1 - side) + 1 - flip
    partner = (1 - upper) * U + unit

    def in_half(r):
        return upper * U + lax.rem(unit + r, U)

    loads = []
    for d in range(D):
        loads.append(pltpu.make_async_copy(att_ref.at[:, d, :], att_v.at[d], sem_l.at[d]))
        loads[-1].start()

    full = N // CHUNK

    def gains(v, a, k, start):
        at = pl.ds(start, CHUNK)
        return (pltpu.make_async_copy(eff_ref.at[at, v, :], eff_v.at[v, a, k], sem_g.at[0, v, a, k]),
                pltpu.make_async_copy(live_ref.at[at, v, :], live_v.at[v, a, k], sem_g.at[1, v, a, k]))

    def load_gains(k, carry):
        for a in range(2):
            c = k * G + group(a, unit)
            for v in range(2):
                @pl.when(c < full)
                def _():
                    for copy in gains(v, a, k, c * CHUNK):
                        copy.start()

                @pl.when(c >= full)
                def _():
                    for copy in gains(v, a, k, N - CHUNK):
                        copy.start()
        return carry

    barrier = pltpu.get_barrier_semaphore()
    greet = [(view, in_half(r)) for r in range(1, U)] + [(across, in_half(r)) for r in range(U)]
    greet += [(beside, slab), (corner, slab), (view, partner)]
    for to in greet:
        pl.semaphore_signal(barrier, inc=1, device_id=to, device_id_type=pl.DeviceIdType.MESH)

    def zero_rows(i, carry):
        nat[i // (square // TILE), pl.ds(pl.multiple_of(i % (square // TILE) * TILE, TILE), TILE), :] = jnp.zeros((TILE, L), f32)
        return carry

    lax.fori_loop(0, D * square // TILE, zero_rows, 0)
    if L > square:
        src[:, :, :, :, square:L] = jnp.zeros((*src.shape[:4], L - square), f32)
    if chunks * CHUNK < image.shape[0]:
        image[chunks * CHUNK:, :] = jnp.zeros((image.shape[0] - chunks * CHUNK, L), f32)
    for d in range(D):
        loads[d].wait()
        if d == D - 1:
            lax.fori_loop(0, K, load_gains, 0)
        nat[d, 0:N, 0:N] = att_v[d]

    pl.semaphore_wait(barrier, len(greet))

    def outgoing(k, r):
        to_unit = lax.rem(unit + r, U)
        g = group(side, to_unit)
        return g, remote(src.at[g, k], slabs_in.at[k, unit], sem_a.at[k, r], sem_ar.at[k, r], view, upper * U + to_unit)

    per_band = LANES // CHUNK
    started = 0
    for b in range(0, square, LANES):
        first = b // CHUNK

        @pl.when(flip == 1)
        def _():
            def act(i, carry):
                c = first + i
                src[c % G, c // G] = nat[:, pl.ds(pl.multiple_of(c * CHUNK, CHUNK), CHUNK), :]
                return carry

            lax.fori_loop(0, per_band, act, 0)

        @pl.when(flip == 0)
        def _():
            def act(d, carry):
                for a in range(0, square, LANES):
                    turned = nat[d, a:a + LANES, b:b + LANES].T
                    for i in range(per_band):
                        c = first + i
                        src[c % G, c // G, d, :, a:a + LANES] = turned[i * CHUNK:(i + 1) * CHUNK, :]
                return carry

            lax.fori_loop(0, D, act, 0)

        while started < K and ((started + 1) * G * CHUNK <= b + LANES or b + LANES == square):
            k = started
            for r in [*range(U // 2, U), *range(1, U // 2)]:
                g, copy = outgoing(k, r)
                guarded(k, g, copy.start)

            def keep_own(k=k):
                slabs_in[k, unit] = src[me, k]

            guarded(k, me, keep_own)
            started += 1

    lane = lax.broadcasted_iota(jnp.int32, (CHUNK, LANES), 1)
    clear = R // LANES * LANES

    def fill(k, carry):
        for a in range(2):
            c = k * G + group(a, unit)
            for v in range(2):
                for copy in gains(v, a, k, N - CHUNK):
                    copy.wait()
                for b in range(clear, L, LANES):
                    blank = jnp.where(lane == LANES - 1, seg_ref[v].astype(f32), 0.0) if b + LANES == L else jnp.zeros((CHUNK, LANES), f32)
                    em[v, a, k, :, b:b + LANES] = blank
                gain = eff_v[v, a, k] * live_v[v, a, k].astype(f32)

                @pl.when(c < full)
                def _():
                    em[v, a, k, :, 0:R] = gain

                if N % CHUNK:
                    @pl.when(c >= full)
                    def _():
                        em[v, a, k, 0:N % CHUNK, 0:R] = gain[CHUNK - N % CHUNK:, :]
        return carry

    lax.fori_loop(0, K, fill, 0)
    em_sends = []
    for r in range(1, 4):
        to_view = lax.rem(view + r, 4)
        em_sends.append(remote(em.at[to_view % 2, to_view // 2], em_in.at[view], sem_e.at[r], sem_er.at[r], to_view, slab))
        em_sends[-1].start()
    em_in[view] = em[flip, side]

    table = [geometry(g, S * D) for g in range(NSEG)]

    def tiles(act):
        def step(t, carry):
            act(pl.ds(pl.multiple_of(t * TILE, TILE), TILE))
            return carry

        if CHUNK == TILE:
            act(slice(0, TILE))
        else:
            lax.fori_loop(0, CHUNK // TILE, step, 0)

    def by_half(act):
        pl.when(upper == 0)(functools.partial(act, 0))
        pl.when(upper == 1)(functools.partial(act, 1))

    def project(k):
        for r in range(1, U):
            from_unit = lax.rem(unit + U - r, U)
            remote(src.at[me, k], slabs_in.at[k, from_unit], sem_a.at[k, r], sem_ar.at[k, r], view, upper * U + from_unit).wait_recv()

        def act(h):
            @tiles
            def _(at):
                for g in range(NSEG):
                    length, taps = table[g]
                    sums = {}
                    for n in range(U * D):
                        m, f = taps[h * U * D + n]
                        plane = slabs_in[k, n // D, n % D, at, :]
                        for shift, coef in ((m, 1.0 - f), (m - 1, f)):
                            term = (length * coef) * plane
                            sums[shift] = sums[shift] + term if shift in sums else term
                    ray = None
                    for shift, value in sums.items():
                        moved = pltpu.roll(value, shift, 1)
                        ray = moved if ray is None else ray + moved
                    mid_out[k, g, at, :] = ray

        by_half(act)

    def mid(k):
        return remote(mid_out.at[k], mid_in.at[k], sem_m.at[k], sem_mr.at[k], view, partner)

    def back_project(k):
        mid(k).wait_recv()
        @tiles
        def _(at):
            for g in range(NSEG):
                gain = jnp.zeros((TILE, L), f32)
                for j in range(4):
                    one = em_in[j, k, at, :]
                    gain = gain + jnp.where(one[:, L - 1:L] == float(g), one, 0.0)
                weights[g, at, :] = table[g][0] * (gain * jnp.exp(-(mid_out[k, g, at, :] + mid_in[k, g, at, :])))

        def act(h):
            @tiles
            def _(at):
                moved = {}

                def shifted(g, m):
                    if (g, m) not in moved:
                        moved[g, m] = pltpu.roll(weights[g, at, :], L - m, 1)
                    return moved[g, m]

                for n in range(U * D):
                    total = None
                    for g in range(NSEG):
                        m, f = table[g][1][h * U * D + n]
                        term = (1.0 - f) * shifted(g, m) + f * shifted(g, m - 1)
                        total = term if total is None else total + term
                    back[k, n // D, n % D, at, :] = total

        by_half(act)
        image[rows_of(k, me), :] = back[k, unit, side]

    def returning(k):
        for r in [*range(U // 2, U), *range(U // 2)]:
            to_unit = lax.rem(unit + r, U)
            for e in range(2):
                if r or e:
                    to_side = (side + e) % 2
                    i = 2 * r + e
                    yield remote(back.at[k, to_unit, to_side], image.at[rows_of(k, me), :], sem_b.at[k, i], sem_br.at[k, i],
                                 2 * to_side + flip, upper * U + to_unit)

    def finish(k):
        back_project(k)
        for copy in returning(k):
            copy.start()

    def arrive(k):
        for r in range(U):
            from_unit = lax.rem(unit + U - r, U)
            for e in range(2):
                if r or e:
                    from_side = (side + e) % 2
                    i = 2 * r + e
                    g = group(from_side, from_unit)
                    copy = remote(back.at[k, unit, side], image.at[rows_of(k, g), :], sem_b.at[k, i], sem_br.at[k, i],
                                  2 * from_side + flip, upper * U + from_unit)
                    guarded(k, g, copy.wait_recv)

    bands = square // LANES
    split = square - LANES
    regions = (
        ((0, half, 0, split, 0), (0, half, split, square, 1)),
        ((half, split, 0, split, 0), (half, split, split, square, 1), (split, 2 * half, 0, square, 1)),
    )
    shared = [min((a + 1) * LANES, half) - a * LANES for a in range(bands) if a * LANES < half]

    def swap(f, a):
        if f == 0:
            lanes = slice(a * LANES, (a + 1) * LANES)
            return remote(part.at[half:2 * half, lanes], other.at[:, lanes], sem_s.at[a], sem_sr.at[a], beside, slab)
        at = slice(a * LANES, a * LANES + shared[a])
        return remote(image.at[at, 0:square], other.at[at, :], sem_s.at[a], sem_sr.at[a], beside, slab)

    def spread(f, i, a_side, sems, to_view):
        r0, r1, l0, l1, _ = regions[f][i]
        place = whole.at[a_side, r0:r1, l0:l1]
        return remote(place, place, sems[0].at[i], sems[1].at[i], to_view, slab)

    def write(f, i, a_side, n):
        r0, r1, l0, l1, _ = regions[f][i]
        return pltpu.make_async_copy(whole.at[a_side, r0:r1, l0:l1], out_ref.at[r0:r1, a_side, l0:l1], sem_w.at[n, i])

    far_sems, near_sems, last_sems = (sem_f, sem_fr), (sem_n, sem_nr), (sem_t, sem_tr)

    def band(f, a):
        if f == 0:
            for b in range(0, square, LANES):
                part[b:b + LANES, a * LANES:(a + 1) * LANES] = image[a * LANES:(a + 1) * LANES, b:b + LANES].T
            swap(0, a).start()
        elif a < len(shared):
            swap(1, a).start()
        if a < bands - 2:
            return
        stage = a - (bands - 2)
        if f == 1:
            for n in range(bands - 1) if stage == 0 else (bands - 1,):
                swap(0, n).wait_recv()
        elif stage == 0:
            for n in range(len(shared)):
                swap(1, n).wait_recv()
        for i, (r0, r1, l0, l1, when) in enumerate(regions[f]):
            if when == stage:
                own = part if f == 0 else image
                whole[side, r0:r1, l0:l1] = own[r0:r1, l0:l1] + other[r0 - f * half:r1 - f * half, l0:l1]
                spread(f, i, side, far_sems, across).start()
                spread(f, i, side, near_sems, beside).start()
                write(f, i, side, 0).start()

    def settle(f):
        for i in range(len(regions[f])):
            spread(f, i, 1 - side, far_sems, across).wait_recv()
            spread(f, i, 1 - side, last_sems, beside).start()
            write(f, i, 1 - side, 1).start()
        for i in range(len(regions[1 - f])):
            spread(1 - f, i, side, near_sems, beside).wait_recv()
            write(1 - f, i, side, 2).start()
        for a in range(bands if f == 0 else len(shared)):
            swap(f, a).wait_send()
        for i in range(len(regions[f])):
            spread(f, i, side, far_sems, across).wait_send()
            spread(f, i, side, near_sems, beside).wait_send()
            write(f, i, side, 0).wait()
        for i in range(len(regions[1 - f])):
            spread(1 - f, i, 1 - side, last_sems, beside).wait_recv()
            write(1 - f, i, 1 - side, 3).start()
        for i in range(len(regions[f])):
            spread(f, i, 1 - side, last_sems, beside).wait_send()
            write(f, i, 1 - side, 1).wait()
        for i in range(len(regions[1 - f])):
            write(1 - f, i, side, 2).wait()
            write(1 - f, i, 1 - side, 3).wait()

    progress = {"arrived": 0, "band": 0}

    def ready(k):
        def act(n, carry):
            arrive(n)
            return carry

        lax.fori_loop(progress["arrived"], k + 1, act, 0)
        progress["arrived"] = k + 1
        while progress["band"] < bands and (k == K - 1 or (progress["band"] + 1) * LANES <= (k + 1) * G * CHUNK):
            for f in range(2):
                pl.when(flip == f)(functools.partial(band, f, progress["band"]))
            progress["band"] += 1

    def step(k, carry):
        @pl.when((k < K) & (k * G + me < chunks))
        def _():
            project(k)
            mid(k).start()

        @pl.when(k == AHEAD)
        def _():
            for r in range(1, 4):
                from_view = lax.rem(view + 4 - r, 4)
                remote(em.at[flip, side], em_in.at[from_view], sem_e.at[r], sem_er.at[r], from_view, slab).wait_recv()

        if K > 1:
            @pl.when(k == K - 1 + AHEAD)
            def _():
                ready(K - 2)

        @pl.when((k >= AHEAD) & ((k - AHEAD) * G + me < chunks))
        def _():
            finish(k - AHEAD)

        return carry

    lax.fori_loop(0, K + AHEAD, step, 0)
    ready(K - 1)

    def drain(k, carry):
        for r in range(1, U):
            g, copy = outgoing(k, r)
            guarded(k, g, copy.wait_send)

        @pl.when(k * G + me < chunks)
        def _():
            mid(k).wait_send()
            for copy in returning(k):
                copy.wait_send()

        return carry

    lax.fori_loop(0, K, drain, 0)
    for copy in em_sends:
        copy.wait_send()
    for f in range(2):
        pl.when(flip == f)(functools.partial(settle, f))


def on_device(atten, view_segment, efficiency, live_mask):
    S = lax.axis_size("slab")
    D, N = atten.shape[0], atten.shape[1]
    R = efficiency.shape[1]
    assert lax.axis_size("view") == 4 and D == 2 and efficiency.shape[0] == 2 and S % 2 == 0
    L = round_up(max(R + 1, N + S * D + 3), LANES)
    square = round_up(N, LANES)
    U = S // 2
    G = 2 * U
    K = -(-N // (G * CHUNK))
    half = round_up(N, 2 * TILE) // 2
    dims = (S, D, N, R, L, K, square, half)
    f32 = jnp.float32
    dma = pltpu.SemaphoreType.DMA
    far = pl.BlockSpec(memory_space=pl.ANY)
    out = pl.pallas_call(
        functools.partial(kernel, dims),
        out_shape=pltpu.VMEM((2 * half, D, square), f32),
        in_specs=[pl.BlockSpec(memory_space=pltpu.SMEM), far, far, far],
        out_specs=pl.BlockSpec(memory_space=pltpu.VMEM),
        scratch_shapes=[
            pltpu.VMEM((D, N, N), f32),
            pltpu.VMEM((2, 2, K, CHUNK, R), f32),
            pltpu.VMEM((2, 2, K, CHUNK, R), jnp.int32),
            pltpu.VMEM((D, square, L), f32),
            pltpu.VMEM((G, max(K, -(-square // (G * CHUNK))), D, CHUNK, L), f32),
            pltpu.VMEM((2, 2, K, CHUNK, L), f32),
            pltpu.VMEM((K, U, D, CHUNK, L), f32),
            pltpu.VMEM((4, K, CHUNK, L), f32),
            pltpu.VMEM((K, NSEG, CHUNK, L), f32),
            pltpu.VMEM((K, NSEG, CHUNK, L), f32),
            pltpu.VMEM((NSEG, CHUNK, L), f32),
            pltpu.VMEM((K, U, D, CHUNK, L), f32),
            pltpu.VMEM((max(K * G * CHUNK, square), L), f32),
            pltpu.VMEM((square, square), f32),
            pltpu.VMEM((half, square), f32),
            pltpu.VMEM((D, 2 * half, square), f32),
            dma((D,)), dma((2, 2, 2, K)),
            dma((K, U)), dma((K, U)), dma((4,)), dma((4,)),
            dma((K,)), dma((K,)), dma((K, G)), dma((K, G)),
            dma((square // LANES,)), dma((square // LANES,)), *[dma((3,))] * 6, dma((4, 3)),
        ],
        compiler_params=pltpu.CompilerParams(collective_id=0, has_side_effects=True, vmem_limit_bytes=61 * 2**20),
    )(view_segment, jnp.transpose(atten, (1, 0, 2)), jnp.transpose(efficiency, (2, 0, 1)), jnp.transpose(live_mask, (2, 0, 1)))
    return jnp.transpose(out[:N, :, :N], (1, 0, 2))


def solution(mesh):
    in_specs = (P("slab", None, None), P("view"), P("view", None, None), P("view", None, None))
    out_specs = P("slab", None, None)
    return jax.shard_map(on_device, mesh=mesh, in_specs=in_specs, out_specs=out_specs, check_vma=False)
```
